512 devices in a mesh: ctx: 64 (over y, x, core), kvh: 8 (over z).
Axes of the slice: x: 4, y: 8, z: 8, core: 2. Of those that a mesh axis runs over, the one named last changes fastest.
Arguments:
- query_states: bfloat16 [65536, 8192], P('ctx', 'kvh')
- key_states: bfloat16 [65536, 1024], P('ctx', 'kvh')
- value_states: bfloat16 [65536, 1024], P('ctx', 'kvh'), may hold values from -6 to 6
- verticals: int32 [8, 4], P('kvh'), may hold values from 0 to 511, as said below
- slashes: int32 [8, 8], P('kvh'), may hold values from 1 to 24, as said below
Outputs:
- attended: bfloat16 [65536, 8192], P(('ctx', 'kvh'))
The draws below stay inside these ranges and needn't reach their ends.
Inputs may be any that keep to these rules, and one draw needn't show every extreme that they name: `verticals`: some head's list holds block 0 and some head's list holds block 511. `slashes`: every head's list holds the offset 24.
All inputs are finite; a program needn't handle non-finite values.
Results may differ from the reference program's by a relative error of at most 0.0049.
Values may be sent and summed in bfloat16 or wider, within the bound.
No kernel may reach another device: no remote copies, remote signals or barrier semaphores. Data moves between devices by JAX's collectives and lax.ppermute only.
A program may use at most 64 MiB of HBM per device.

```python
import jax
import jax.numpy as jnp
from jax import lax

HD = 128
GROUP = 8
BLK = 128
NV = 4
NS = 8
KVH = 8
QH = 64
TOKENS = 65536
NB = 512
SMAX = 24
NCAND = 13


def shared_keys(key):
    return jax.random.normal(jax.random.fold_in(key, 11), (TOKENS, KVH * HD), jnp.float32)


def draw_key_states(key, part):
    shared = shared_keys(key)
    return shared.astype(jnp.bfloat16)


def draw_query_states(key, part):
    key = jax.random.fold_in(key, 2)
    queries = jax.random.normal(key, (TOKENS, QH * HD), jnp.float32)
    return queries.astype(jnp.bfloat16)


def draw_verticals(key, part):
    key = jax.random.fold_in(key, 4)
    first = jax.random.randint(jax.random.fold_in(key, 1), (KVH, NV), 0, NB)
    second = jax.random.randint(jax.random.fold_in(key, 2), (KVH, NV), 0, NB)
    third = jax.random.randint(jax.random.fold_in(key, 3), (KVH, NV), 0, NB)
    picks = jnp.minimum(jnp.minimum(first, second), third)
    top_head = jax.random.randint(jax.random.fold_in(key, 5), (), 0, KVH)
    top_column = jax.random.randint(jax.random.fold_in(key, 6), (), 0, NV)
    low_head = jax.random.randint(jax.random.fold_in(key, 7), (), 0, KVH)
    low_column = (top_column + 1) % NV
    heads = jnp.arange(KVH, dtype=jnp.int32)[:, None]
    columns = jnp.arange(NV, dtype=jnp.int32)[None, :]
    picks = jnp.where((heads == top_head) & (columns == top_column), NB - 1, picks)
    picks = jnp.where((heads == low_head) & (columns == low_column), 0, picks)
    return picks.astype(jnp.int32)


def draw_slashes(key, part):
    key = jax.random.fold_in(key, 3)
    offsets = jax.random.randint(jax.random.fold_in(key, 1), (KVH, NS), 1, SMAX + 1)
    which_column = jax.random.randint(jax.random.fold_in(key, 2), (KVH,), 0, NS)
    columns = jnp.arange(NS, dtype=jnp.int32)[None, :]
    return jnp.where(columns == which_column[:, None], SMAX, offsets).astype(jnp.int32)


def block_levels(key, extent, cuts, least, largest):
    factor_of, own = 1.0, jax.random.fold_in(key, 6)
    for axis_at, blocks in cuts:
        heights = jnp.exp(jax.random.uniform(jax.random.fold_in(own, axis_at), (blocks,), jnp.float32, least / len(cuts), largest / len(cuts)))
        factor_of = factor_of * jnp.repeat(heights, extent[axis_at] // blocks).reshape([-1 if axis == axis_at else 1 for axis in range(len(extent))])
    return factor_of


def normal_values(key, shape, deviation, most, shards=(), kind=jnp.bfloat16):
    factor_of = block_levels(key, shape, shards, -0.22, 0.18) if shards else 1.0
    array = jax.random.normal(key, shape, jnp.float32) * deviation * factor_of
    return jnp.minimum(jnp.maximum(array, -most), most).astype(kind)


def setup_inputs(seed: int = 0) -> dict:
    keys = jax.random.split(jax.random.key(seed), 6)
    return {
        "query_states": draw_query_states(jax.random.fold_in(keys[5], 71), 0),
        "key_states": draw_key_states(jax.random.fold_in(keys[5], 71), 0),
        "value_states": normal_values(keys[2], (TOKENS, KVH * HD), 1.0, 6.0, ((0, 64), (1, 8))),
        "verticals": draw_verticals(jax.random.fold_in(keys[5], 71), 0),
        "slashes": draw_slashes(jax.random.fold_in(keys[5], 71), 0),
    }


def candidates(block_now, slash_row, vert_row):
    block_ids = jnp.concatenate([block_now[None], block_now - slash_row, vert_row]).astype(jnp.int32)
    count = block_ids.shape[0]
    order = jnp.arange(count, dtype=jnp.int32)
    same_id = block_ids[:, None] == block_ids[None, :]
    earlier = order[None, :] < order[:, None]
    repeated = jnp.any(same_id & earlier, axis=1)
    live = (block_ids >= 0) & (block_ids <= block_now) & jnp.logical_not(repeated)
    return block_ids, live


def attend_block(query_block, key_cand, value_cand, live):
    scores = jnp.einsum("tgd,kd->gtk", query_block.astype(jnp.float32), key_cand.astype(jnp.float32)) * (HD ** -0.5)
    width = key_cand.shape[0]
    query_pos = lax.broadcasted_iota(jnp.int32, (BLK, width), 0)
    key_pos = lax.broadcasted_iota(jnp.int32, (BLK, width), 1)
    cand_index = key_pos // BLK
    within = key_pos % BLK
    allowed = live[cand_index] & ((cand_index > 0) | (within <= query_pos))
    masked = jnp.where(allowed[None], scores, -1e30)
    row_max = jnp.max(masked, axis=-1, keepdims=True)
    numerator = jnp.where(allowed[None], jnp.exp(masked - row_max), 0.0)
    row_total = jnp.sum(numerator, axis=-1, keepdims=True)
    weights = (numerator / row_total).astype(jnp.bfloat16)
    result = jnp.einsum("gtk,kd->tgd", weights.astype(jnp.float32), value_cand.astype(jnp.float32))
    return result.astype(jnp.bfloat16)


def reference(query_states, key_states, value_states, verticals, slashes):
    query_blocks = query_states.reshape(NB, BLK, KVH, GROUP, HD)
    key_blocks = key_states.reshape(NB, BLK, KVH, HD)
    value_blocks = value_states.reshape(NB, BLK, KVH, HD)

    def attend_one(pair_id):
        group_id = pair_id // NB
        block_now = pair_id % NB
        block_ids, live = candidates(block_now, slashes[group_id], verticals[group_id])
        safe_ids = jnp.clip(block_ids, 0, NB - 1)
        key_group = lax.dynamic_index_in_dim(key_blocks, group_id, axis=2, keepdims=False)
        value_group = lax.dynamic_index_in_dim(value_blocks, group_id, axis=2, keepdims=False)
        key_cand = key_group[safe_ids].reshape(NCAND * BLK, HD)
        value_cand = value_group[safe_ids].reshape(NCAND * BLK, HD)
        query_block = lax.dynamic_index_in_dim(query_blocks[block_now], group_id, axis=1, keepdims=False)
        return attend_block(query_block, key_cand, value_cand, live)

    outputs = lax.map(attend_one, jnp.arange(KVH * NB, dtype=jnp.int32))
    outputs = outputs.reshape(KVH, NB, BLK, GROUP, HD).transpose(1, 2, 0, 3, 4)
    return outputs.reshape(TOKENS, QH * HD)
```

```python
import functools

import jax
import jax.numpy as jnp
from jax import lax
from jax.experimental import pallas as pl
from jax.experimental.pallas import tpu as pltpu
from jax.sharding import PartitionSpec as P

HD = 128
BLK = 128
REACH = 3
FAR = -1e30
EXP2_SCALE = HD ** (-0.5) * 1.4426950408889634
CALLS = ((3,), (-3,), (4, 2), (-2, 1), (-1, 0))


def candidates(block_now, slash_row, vert_row):
    block_ids = jnp.concatenate([block_now[None], block_now - slash_row, vert_row])
    count = block_ids.shape[0]
    order = jnp.arange(count, dtype=jnp.int32)
    same_id = block_ids[:, None] == block_ids[None, :]
    earlier = order[None, :] < order[:, None]
    repeated = jnp.any(same_id & earlier, axis=1)
    live = (block_ids >= 0) & (block_ids <= block_now) & jnp.logical_not(repeated)
    return live


def attend_kernel(offsets, slash_count, vert_count, live_ref, place_ref, pick_ref, query_ref, *refs):
    sources = refs[:4]
    columns_ref = refs[4]
    count = len(offsets)
    outs = refs[6 : 6 + count]
    query_buf, kv_buf, live_buf, sems = refs[6 + count :]
    cand_count = 1 + slash_count + vert_count

    def fetch(at):
        block = pick_ref[offsets[at]]
        row = pl.multiple_of(block * BLK, BLK)
        pltpu.make_async_copy(query_ref.at[pl.ds(row, BLK), :], query_buf.at[at], sems.at[at, 0]).start()
        pltpu.make_async_copy(
            sources[0].at[:, pl.ds(row, BLK), :], kv_buf.at[at, :, pl.ds(0, BLK), :], sems.at[at, 1]
        ).start()
        for k in range(slash_count):
            place = place_ref[block, k]
            which = place // 8
            from_row = pl.multiple_of((place % 8) * BLK, BLK)
            for number in range(4):

                @pl.when(which == number)
                def _(number=number, k=k, from_row=from_row):
                    pltpu.make_async_copy(
                        sources[number].at[:, pl.ds(from_row, BLK), :],
                        kv_buf.at[at, :, pl.ds((1 + k) * BLK, BLK), :],
                        sems.at[at, 1],
                    ).start()

        pltpu.make_async_copy(
            columns_ref, kv_buf.at[at, :, pl.ds((1 + slash_count) * BLK, vert_count * BLK), :], sems.at[at, 1]
        ).start()

    def settle(at):
        block = pick_ref[offsets[at]]
        pltpu.make_async_copy(query_buf.at[at], query_buf.at[at], sems.at[at, 0]).wait()
        pltpu.make_async_copy(kv_buf.at[at], kv_buf.at[at], sems.at[at, 1]).wait()
        live_buf[at, pl.ds(0, BLK), :] = jnp.ones((BLK, HD), jnp.bfloat16)
        first_key = kv_buf[at, 0, pl.ds(0, 1), :]
        for c in range(1, cand_count):
            rows = pl.ds(c * BLK, BLK)
            alive = live_ref[block, c]

            @pl.when(alive != 0)
            def _(rows=rows):
                live_buf[at, rows, :] = jnp.ones((BLK, HD), jnp.bfloat16)

            @pl.when(alive == 0)
            def _(rows=rows):
                kv_buf[at, 0, rows, :] = jnp.broadcast_to(first_key, (BLK, HD))
                kv_buf[at, 1, rows, :] = jnp.zeros((BLK, HD), jnp.bfloat16)
                live_buf[at, rows, :] = jnp.zeros((BLK, HD), jnp.bfloat16)

    def attend(at):
        heads = query_buf.shape[2] // HD
        within = lax.broadcasted_iota(jnp.int32, (BLK, BLK), 0) >= lax.broadcasted_iota(jnp.int32, (BLK, BLK), 1)
        within = jnp.concatenate([within, within], axis=0)
        for h in range(0, heads, 2):
            left = query_buf[at, :, pl.ds(h * HD, HD)]
            right = query_buf[at, :, pl.ds((h + 1) * HD, HD)]
            both = jnp.concatenate([left, right], axis=0)
            scores = lax.dot_general(
                both, kv_buf[at, 0], (((1,), (1,)), ((), ())), preferred_element_type=jnp.float32
            )
            own = jnp.where(within, scores[:, :BLK], FAR)
            scores = jnp.concatenate([own, scores[:, BLK:]], axis=1)
            row_max = jnp.max(scores, axis=1, keepdims=True)
            weights = jnp.exp2((scores - row_max) * EXP2_SCALE).astype(jnp.bfloat16)
            widened = jnp.concatenate([kv_buf[at, 1], live_buf[at]], axis=1)
            total = jnp.dot(weights, widened, preferred_element_type=jnp.float32)
            result = (total[:, :HD] / total[:, HD:]).astype(jnp.bfloat16)
            outs[at][:, pl.ds(h * HD, HD)] = result[:BLK]
            outs[at][:, pl.ds((h + 1) * HD, HD)] = result[BLK:]

    for at in range(count):
        fetch(at)
    for at in range(count):
        settle(at)
        attend(at)


def attend_call(offsets, live, place, pick, query, sources, columns, previous):
    count = len(offsets)
    slash_count = place.shape[1]
    vert_count = columns.shape[1] // BLK
    width = (1 + slash_count + vert_count) * BLK
    columns_of_query = query.shape[1]
    rows = BLK * columns_of_query // HD
    anywhere = pl.BlockSpec(memory_space=pl.ANY)
    scalars = pl.BlockSpec(memory_space=pltpu.SMEM)
    return pl.pallas_call(
        functools.partial(attend_kernel, offsets, slash_count, vert_count),
        out_shape=[jax.ShapeDtypeStruct((BLK, columns_of_query), jnp.bfloat16)] * count,
        in_specs=[scalars] * 3 + [anywhere] * 7,
        out_specs=[pl.BlockSpec(memory_space=pltpu.VMEM)] * count,
        scratch_shapes=[
            pltpu.VMEM((count, BLK, columns_of_query), jnp.bfloat16),
            pltpu.VMEM((count, 2, width, HD), jnp.bfloat16),
            pltpu.VMEM((count, width, HD), jnp.bfloat16),
            pltpu.SemaphoreType.DMA((count, 2)),
        ],
        compiler_params=pltpu.CompilerParams(vmem_limit_bytes=40 * 2**20),
        cost_estimate=pl.CostEstimate(
            flops=count * 4 * rows * width * HD, bytes_accessed=count * 2**20, transcendentals=count * rows * width
        ),
    )(live, place, pick, query, *sources, columns, previous)


def assemble_kernel(count, start_ref, *refs):
    pieces, out_ref, sems = refs[:count], refs[count], refs[count + 1]
    width = pieces[0].shape[1]
    copies = []
    for n in range(count):
        at = pl.multiple_of(start_ref[n] * width, width)
        copies.append(pltpu.make_async_copy(pieces[n], out_ref.at[:, pl.ds(at, width)], sems.at[n]))
        copies[-1].start()
    for copy in copies:
        copy.wait()


def assemble(starts, pieces):
    count = len(pieces)
    rows, width = pieces[0].shape
    anywhere = pl.BlockSpec(memory_space=pl.ANY)
    return pl.pallas_call(
        functools.partial(assemble_kernel, count),
        out_shape=jax.ShapeDtypeStruct((rows, count * width), jnp.bfloat16),
        in_specs=[pl.BlockSpec(memory_space=pltpu.SMEM)] + [anywhere] * count,
        out_specs=anywhere,
        scratch_shapes=[pltpu.SemaphoreType.DMA((count,))],
        cost_estimate=pl.CostEstimate(flops=0, bytes_accessed=4 * rows * count * width, transcendentals=0),
    )(starts, *pieces)


def shards(query_states, key_states, value_states, verticals, slashes):
    stretch = key_states.shape[0]
    blocks = stretch // BLK
    stretches = lax.axis_size("ctx")
    planes = lax.axis_size("kvh")
    rank_ctx = lax.axis_index("ctx")
    rank_kvh = lax.axis_index("kvh")
    vert_row = verticals[0]
    slash_row = slashes[0]

    key_value = jnp.stack([key_states, value_states])
    owners = vert_row // blocks
    local_slot = jnp.clip(vert_row - rank_ctx * blocks, 0, blocks - 1)
    picked = key_value.reshape(2, blocks, BLK, HD)[:, local_slot]
    picked = jnp.where((owners == rank_ctx)[None, :, None, None], picked, jnp.zeros((), jnp.bfloat16))
    columns = lax.psum(picked, "ctx").reshape(2, -1, HD)

    ring = range(stretches)
    two_back = lax.ppermute(key_value, "ctx", [(s, (s + 2) % stretches) for s in ring])
    mixed = lax.ppermute(key_value, "ctx", [(s, (s + (1 if s % 2 == 0 else 3)) % stretches) for s in ring])
    swapped = lax.ppermute(two_back, "ctx", [(s, s ^ 1) for s in ring])
    sources = (key_value, swapped, two_back, mixed)

    local = jnp.arange(blocks, dtype=jnp.int32)
    live = jax.vmap(lambda block: candidates(block, slash_row, vert_row))(rank_ctx * blocks + local)
    live = live.astype(jnp.int32)
    relative = local[:, None] - slash_row[None, :]
    hops = (blocks - 1 - relative) // blocks
    odd = rank_ctx % 2 == 1
    which = jnp.where(odd & (hops > 0), REACH + 1 - hops, hops)
    place = which * blocks + (relative + REACH * blocks) % blocks
    pick = (rank_kvh + local) % planes

    pieces = []
    starts = []
    previous = key_value
    for offsets in CALLS:
        wanted = tuple(offset % planes for offset in offsets)
        results = attend_call(wanted, live, place, pick, query_states, sources, columns, previous)
        previous = results[0]
        for offset, result in zip(wanted, results):
            if offset:
                result = lax.ppermute(result, "kvh", [(s, (s + offset) % planes) for s in range(planes)])
            pieces.append(result)
            starts.append((rank_kvh - offset) % planes)
    return assemble(jnp.stack(starts).astype(jnp.int32), pieces)


def solution(mesh):
    return jax.shard_map(
        shards,
        mesh=mesh,
        in_specs=(
            P("ctx", "kvh"),
            P("ctx", "kvh"),
            P("ctx", "kvh"),
            P("kvh", None),
            P("kvh", None),
        ),
        out_specs=P(("ctx", "kvh"), None),
        check_vma=False,
    )
```

```python
import functools

import jax
import jax.numpy as jnp
from jax import lax
from jax.experimental import pallas as pl
from jax.experimental.pallas import tpu as pltpu
from jax.sharding import PartitionSpec as P

HD = 128
BLK = 128
REACH = 3
FAR = -1e30
EXP2_SCALE = HD ** (-0.5) * 1.4426950408889634
VMEM_BYTES = 62 * 2**20
KEY_TILE = 256
ROW_TILE = 16
CALLS = ((3,), (-3,), (2, 4), (1, -2), (-1, 0))

ANYWHERE = pl.BlockSpec(memory_space=pl.ANY)
SCALARS = pl.BlockSpec(memory_space=pltpu.SMEM)
IN_VMEM = pl.BlockSpec(memory_space=pltpu.VMEM)
LIMITS = pltpu.CompilerParams(vmem_limit_bytes=VMEM_BYTES)


def small_cost(bytes_accessed):
    return pl.CostEstimate(flops=0, bytes_accessed=bytes_accessed, transcendentals=0)


def prepare_kernel(where_ref, verticals_ref, keys_ref, values_ref, stacked_ref, picked_ref, sems):
    copies = [
        pltpu.make_async_copy(keys_ref, stacked_ref.at[0], sems.at[0]),
        pltpu.make_async_copy(values_ref, stacked_ref.at[1], sems.at[1]),
    ]
    for copy in copies:
        copy.start()
    for copy in copies:
        copy.wait()
    blocks = keys_ref.shape[0] // BLK
    for v in range(verticals_ref.shape[1]):
        block = verticals_ref[0, v]
        mine = block // blocks == where_ref[0]
        row = pl.multiple_of((block % blocks) * BLK, BLK)
        rows = pl.ds(v * BLK, BLK)

        @pl.when(mine)
        def _(row=row, rows=rows):
            picked_ref[:, rows, :] = stacked_ref[:, pl.ds(row, BLK), :]

        @pl.when(jnp.logical_not(mine))
        def _(rows=rows):
            picked_ref[:, rows, :] = jnp.zeros((2, BLK, HD), jnp.bfloat16)


def prepare(where, verticals, keys, values):
    stretch = keys.shape[0]
    return pl.pallas_call(
        prepare_kernel,
        out_shape=[
            jax.ShapeDtypeStruct((2, stretch, HD), jnp.bfloat16),
            jax.ShapeDtypeStruct((2, verticals.shape[1] * BLK, HD), jnp.bfloat16),
        ],
        in_specs=[SCALARS, SCALARS, ANYWHERE, ANYWHERE],
        out_specs=[IN_VMEM, IN_VMEM],
        scratch_shapes=[pltpu.SemaphoreType.DMA((2,))],
        compiler_params=LIMITS,
        cost_estimate=small_cost(2**20),
    )(where, verticals, keys, values)


def attend_kernel(offsets, blocks, where_ref, verticals_ref, slashes_ref, query_ref, *refs):
    sources = refs[:4]
    columns_ref = refs[4]
    count = len(offsets)
    outs, scratch = refs[-8 - count : -8], refs[-8:]
    query_buf, kv_buf, live_buf, scores_even, scores_odd, weights_even, weights_odd, sems = scratch
    slash_count = slashes_ref.shape[1]
    vert_count = verticals_ref.shape[1]
    cand_count = 1 + slash_count + vert_count
    width = cand_count * BLK
    heads = query_buf.shape[2] // HD
    score_bufs = (scores_even, scores_odd)
    weight_bufs = (weights_even, weights_odd)
    rank_ctx = where_ref[0]
    odd = rank_ctx % 2

    def local_block(at):
        return (where_ref[1] + offsets[at]) % blocks

    def fetch(at):
        block = local_block(at)
        row = pl.multiple_of(block * BLK, BLK)
        pltpu.make_async_copy(query_ref.at[pl.ds(row, BLK), :], query_buf.at[at], sems.at[at, 0]).start()
        pltpu.make_async_copy(
            sources[0].at[:, pl.ds(row, BLK), :], kv_buf.at[at, :, pl.ds(0, BLK), :], sems.at[at, 1]
        ).start()
        for k in range(slash_count):
            relative = block - slashes_ref[0, k] + REACH * blocks
            hops = REACH - relative // blocks
            which = jnp.where((odd == 1) & (hops > 0), REACH + 1 - hops, hops)
            from_row = pl.multiple_of((relative % blocks) * BLK, BLK)
            for number in range(4):

                @pl.when(which == number)
                def _(number=number, k=k, from_row=from_row):
                    pltpu.make_async_copy(
                        sources[number].at[:, pl.ds(from_row, BLK), :],
                        kv_buf.at[at, :, pl.ds((1 + k) * BLK, BLK), :],
                        sems.at[at, 1],
                    ).start()

        pltpu.make_async_copy(
            columns_ref, kv_buf.at[at, :, pl.ds((1 + slash_count) * BLK, vert_count * BLK), :], sems.at[at, 1]
        ).start()

    def settle(at):
        block_now = rank_ctx * blocks + local_block(at)
        ids = [block_now]
        ids += [block_now - slashes_ref[0, k] for k in range(slash_count)]
        ids += [verticals_ref[0, k] for k in range(vert_count)]
        pltpu.make_async_copy(query_buf.at[at], query_buf.at[at], sems.at[at, 0]).wait()
        pltpu.make_async_copy(kv_buf.at[at], kv_buf.at[at], sems.at[at, 1]).wait()
        live_buf[at, pl.ds(0, BLK), :] = jnp.ones((BLK, HD), jnp.bfloat16)
        for c in range(1, cand_count):
            alive = (ids[c] >= 0) & (ids[c] <= block_now)
            for earlier in range(c):
                alive = alive & (ids[c] != ids[earlier])
            rows = pl.ds(c * BLK, BLK)
            live_buf[at, rows, :] = jnp.broadcast_to(jnp.where(alive, 1.0, 0.0), (BLK, HD)).astype(jnp.bfloat16)

            @pl.when(jnp.logical_not(alive))
            def _(rows=rows):
                first_key = kv_buf[at, 0, pl.ds(0, 1), :]
                kv_buf[at, 0, rows, :] = jnp.broadcast_to(first_key, (BLK, HD))
                kv_buf[at, 1, rows, :] = jnp.zeros((BLK, HD), jnp.bfloat16)

    def score_steps(at, pair):
        def step(start):
            size = min(KEY_TILE, width - start)
            left = query_buf[at, :, pl.ds(2 * pair * HD, HD)]
            right = query_buf[at, :, pl.ds((2 * pair + 1) * HD, HD)]
            score_bufs[pair % 2][:, pl.ds(start, size)] = lax.dot_general(
                jnp.concatenate([left, right], axis=0),
                kv_buf[at, 0, pl.ds(start, size), :],
                (((1,), (1,)), ((), ())),
                preferred_element_type=jnp.float32,
            )

        return [functools.partial(step, start) for start in range(0, width, KEY_TILE)]

    def weight_steps(pair):
        def step(start):
            rows = pl.ds(start, ROW_TILE)
            scores = score_bufs[pair % 2][rows, :]
            position = lax.broadcasted_iota(jnp.int32, (ROW_TILE, BLK), 0) + start % BLK
            within = position >= lax.broadcasted_iota(jnp.int32, (ROW_TILE, BLK), 1)
            own = jnp.where(within, scores[:, :BLK], FAR)
            scores = jnp.concatenate([own, scores[:, BLK:]], axis=1)
            row_max = jnp.max(scores, axis=1, keepdims=True)
            weights = jnp.exp2((scores - row_max) * EXP2_SCALE)
            weight_bufs[pair % 2][rows, :] = weights.astype(jnp.bfloat16)

        return [functools.partial(step, start) for start in range(0, 2 * BLK, ROW_TILE)]

    def value_step(at, pair):
        widened = jnp.concatenate([kv_buf[at, 1], live_buf[at]], axis=1)
        total = jnp.dot(weight_bufs[pair % 2][...], widened, preferred_element_type=jnp.float32)
        result = (total[:, :HD] / total[:, HD:]).astype(jnp.bfloat16)
        outs[at][:, pl.ds(2 * pair * HD, HD)] = result[:BLK]
        outs[at][:, pl.ds((2 * pair + 1) * HD, HD)] = result[BLK:]

    def attend(at):
        pairs = heads // 2
        for step in score_steps(at, 0):
            step()
        for pair in range(pairs):
            products = [functools.partial(value_step, at, pair - 1)] if pair else []
            products += score_steps(at, pair + 1) if pair + 1 < pairs else []
            weights = weight_steps(pair)
            every = max(1, len(weights) // max(1, len(products)))
            for n, step in enumerate(weights):
                if n % every == 0 and products:
                    products.pop(0)()
                step()
            for step in products:
                step()
        value_step(at, pairs - 1)

    for at in range(count):
        fetch(at)
    for at in range(count):
        settle(at)
        attend(at)


def attend_call(offsets, blocks, where, verticals, slashes, query, sources, columns, after):
    count = len(offsets)
    width = (1 + slashes.shape[1] + verticals.shape[1]) * BLK
    query_width = query.shape[1]
    return pl.pallas_call(
        functools.partial(attend_kernel, offsets, blocks),
        out_shape=[jax.ShapeDtypeStruct((BLK, query_width), jnp.bfloat16)] * count,
        in_specs=[SCALARS] * 3 + [ANYWHERE] * (6 + len(after)),
        out_specs=[IN_VMEM] * count,
        scratch_shapes=[
            pltpu.VMEM((count, BLK, query_width), jnp.bfloat16),
            pltpu.VMEM((count, 2, width, HD), jnp.bfloat16),
            pltpu.VMEM((count, width, HD), jnp.bfloat16),
            pltpu.VMEM((2 * BLK, width), jnp.float32),
            pltpu.VMEM((2 * BLK, width), jnp.float32),
            pltpu.VMEM((2 * BLK, width), jnp.bfloat16),
            pltpu.VMEM((2 * BLK, width), jnp.bfloat16),
            pltpu.SemaphoreType.DMA((count, 2)),
        ],
        compiler_params=LIMITS,
        cost_estimate=pl.CostEstimate(
            flops=4 * count * BLK * query_width * width,
            bytes_accessed=count * 2**20,
            transcendentals=count * BLK * query_width // HD * width,
        ),
    )(where, verticals, slashes, query, *sources, columns, *after)


def assemble_kernel(offsets, where_ref, *refs):
    count = len(offsets)
    pieces, out_ref, sems = refs[:count], refs[count], refs[count + 1]
    width = pieces[0].shape[1]
    copies = []
    for n, offset in enumerate(offsets):
        source = (where_ref[1] + count - offset) % count
        at = pl.multiple_of(source * width, width)
        copies.append(pltpu.make_async_copy(pieces[n], out_ref.at[:, pl.ds(at, width)], sems.at[n]))
        copies[-1].start()
    for copy in copies:
        copy.wait()


def assemble(offsets, where, pieces):
    count = len(pieces)
    rows, width = pieces[0].shape
    return pl.pallas_call(
        functools.partial(assemble_kernel, offsets),
        out_shape=jax.ShapeDtypeStruct((rows, count * width), jnp.bfloat16),
        in_specs=[SCALARS] + [ANYWHERE] * count,
        out_specs=IN_VMEM,
        scratch_shapes=[pltpu.SemaphoreType.DMA((count,))],
        compiler_params=LIMITS,
        cost_estimate=small_cost(4 * rows * count * width),
    )(where, *pieces)


def window_routes(stretches):
    chips = stretches // 2
    first, mixed, last = [], [], []
    for chip in range(chips):
        y, x = divmod(chip, 4)
        for core in range(2):
            first.append((2 * chip + core, (2 * chip + core + 2) % stretches))
        mixed.append((2 * chip, 2 * chip + 1))
        half_y = y + 1 if x == 2 else y
        half = (half_y * 4 + (x - 1) % 4) % chips
        target = (chip + 2) % chips
        mixed.append((2 * chip + 1, 2 * half))
        last.append((2 * half, 2 * target))
    return first, mixed, last


def shards(query_states, key_states, value_states, verticals, slashes):
    stretch = key_states.shape[0]
    blocks = stretch // BLK
    stretches = lax.axis_size("ctx")
    planes = lax.axis_size("kvh")
    where = jnp.stack([lax.axis_index("ctx"), lax.axis_index("kvh")]).astype(jnp.int32)
    key_value, picked = prepare(where, verticals, key_states, value_states)

    first, mixed, last = window_routes(stretches)
    two_back = lax.ppermute(key_value, "ctx", first)
    halfway = lax.ppermute(key_value, "ctx", mixed)

    shares = picked.reshape(stretches, -1, HD)
    shares = lax.all_to_all(shares, "ctx", split_axis=0, concat_axis=0, tiled=True)
    share = jnp.sum(shares.astype(jnp.float32), axis=0).astype(jnp.bfloat16)
    share, two_back = lax.optimization_barrier((share, two_back))
    swapped = lax.ppermute(two_back, "ctx", [(s, s ^ 1) for s in range(stretches)])
    onward = lax.ppermute(halfway, "ctx", last)
    shares = jnp.broadcast_to(share[None], (stretches,) + share.shape)
    columns = lax.all_to_all(shares, "ctx", split_axis=0, concat_axis=0, tiled=True).reshape(2, -1, HD)
    near = jnp.where(where[0] % 2 == 1, halfway, onward)
    sources = (key_value, swapped, two_back, near)

    pieces = []
    came = []
    after = []
    for number, offsets in enumerate(CALLS):
        wanted = tuple(offset % planes for offset in offsets)
        if number == len(CALLS) - 1:
            after = after + pieces[:2]
        results = attend_call(wanted, blocks, where, verticals, slashes, query_states, sources, columns, after)
        after = [results[0]]
        for offset, result in zip(wanted, results):
            if offset:
                result = lax.ppermute(result, "kvh", [(s, (s + offset) % planes) for s in range(planes)])
            pieces.append(result)
            came.append(offset)
    return assemble(tuple(came), where, pieces)


def solution(mesh):
    return jax.shard_map(
        shards,
        mesh=mesh,
        in_specs=(
            P("ctx", "kvh"),
            P("ctx", "kvh"),
            P("ctx", "kvh"),
            P("kvh", None),
            P("kvh", None),
        ),
        out_specs=P(("ctx", "kvh"), None),
        check_vma=False,
    )
```

```python
import functools

import jax
import jax.numpy as jnp
from jax import lax
from jax.experimental import pallas as pl
from jax.experimental.pallas import tpu as pltpu
from jax.sharding import PartitionSpec as P

HD = 128
BLK = 128
REACH = 3
ONES = 16
FAR = -1e30
EXP2_SCALE = HD ** (-0.5) * 1.4426950408889634
VMEM_BYTES = 32 * 2**20
PAIR = 2
CALLS = ((3,), (-3,), (4,), (2,), (-2,), (1,), (-1,), (0,))
ARRIVED = {5: (0,), 6: (1,), 7: (2,)}
ROW = 8

ANYWHERE = pl.BlockSpec(memory_space=pl.ANY)
SCALARS = pl.BlockSpec(memory_space=pltpu.SMEM)
IN_VMEM = pl.BlockSpec(memory_space=pltpu.VMEM)
LIMITS = pltpu.CompilerParams(vmem_limit_bytes=VMEM_BYTES)
SMALL = pltpu.CompilerParams(vmem_limit_bytes=8 * 2**20)
MOST_VMEM = pltpu.CompilerParams(vmem_limit_bytes=60 * 2**20)


def small_cost(bytes_accessed):
    return pl.CostEstimate(flops=0, bytes_accessed=bytes_accessed, transcendentals=0)


def prepare_kernel(verticals_ref, keys_ref, values_ref, stacked_ref, picked_ref, verticals_buf, values_buf, sems):
    verticals_in = pltpu.make_async_copy(verticals_ref, verticals_buf, sems.at[0])
    values_in = pltpu.make_async_copy(values_ref, values_buf, sems.at[1])
    keys_in = pltpu.make_async_copy(keys_ref, stacked_ref.at[0], sems.at[2])
    values_in.start()
    keys_in.start()
    verticals_in.start()
    blocks = keys_ref.shape[0] // BLK
    values_in.wait()
    for j in range(blocks):
        rows = pl.ds(j * BLK, BLK)
        stacked_ref[1, rows, :] = values_buf[rows, :].T
    keys_in.wait()
    verticals_in.wait()
    for v in range(verticals_ref.shape[1]):
        block = verticals_buf[0, v]
        mine = lax.div(block, blocks) == lax.axis_index("ctx")
        row = pl.multiple_of(lax.rem(block, blocks) * BLK, BLK)
        rows = pl.ds(v * BLK, BLK)

        @pl.when(mine)
        def _(row=row, rows=rows):
            picked_ref[:, rows, :] = stacked_ref[:, pl.ds(row, BLK), :]

        @pl.when(jnp.logical_not(mine))
        def _(rows=rows):
            picked_ref[:, rows, :] = jnp.zeros((2, BLK, HD), jnp.bfloat16)


def prepare(verticals, keys, values):
    stretch = keys.shape[0]
    return pl.pallas_call(
        prepare_kernel,
        out_shape=[
            jax.ShapeDtypeStruct((2, stretch, HD), jnp.bfloat16),
            jax.ShapeDtypeStruct((2, verticals.shape[1] * BLK, HD), jnp.bfloat16),
        ],
        in_specs=[ANYWHERE] * 3,
        out_specs=[IN_VMEM, IN_VMEM],
        scratch_shapes=[
            pltpu.SMEM(verticals.shape, jnp.int32),
            pltpu.VMEM((stretch, HD), jnp.bfloat16),
            pltpu.SemaphoreType.DMA((3,)),
        ],
        compiler_params=MOST_VMEM,
        cost_estimate=small_cost(2**20),
    )(verticals, keys, values)


def plan_kernel(blocks, verticals_ref, slashes_ref, slots_ref):
    slash_count = slashes_ref.shape[1]
    vert_count = verticals_ref.shape[1]
    count = 1 + slash_count + vert_count
    rank_ctx = lax.axis_index("ctx")

    def one(local, _):
        block_now = rank_ctx * blocks + local
        ids = [block_now]
        ids += [block_now - slashes_ref[0, k] for k in range(slash_count)]
        ids += [verticals_ref[0, k] for k in range(vert_count)]
        base = REACH * blocks
        slots = [base + local]
        slots += [base + local - slashes_ref[0, k] for k in range(slash_count)]
        slots += [base + blocks + k for k in range(vert_count)]
        dead = base + blocks + vert_count + local
        slots_ref[local * count] = slots[0]
        for c in range(1, count):
            alive = (ids[c] >= 0) & (ids[c] <= block_now)
            for earlier in range(c):
                alive = alive & (ids[c] != ids[earlier])
            slots_ref[local * count + c] = jnp.where(alive, slots[c], dead)
        return 0

    lax.fori_loop(0, blocks, one, 0)


def plan(blocks, verticals, slashes):
    count = 1 + slashes.shape[1] + verticals.shape[1]
    return pl.pallas_call(
        functools.partial(plan_kernel, blocks),
        out_shape=jax.ShapeDtypeStruct((blocks * count,), jnp.int32),
        in_specs=[SCALARS] * 2,
        out_specs=SCALARS,
        compiler_params=SMALL,
        cost_estimate=small_cost(2**20),
    )(verticals, slashes)


def pool_kernel(blocks, own_ref, swapped_ref, two_ref, halfway_ref, onward_ref, columns_ref, pool_ref, sems):
    odd = lax.rem(lax.axis_index("ctx"), 2)
    rows = blocks * BLK

    def copy(source, stretch_at, number):
        return pltpu.make_async_copy(
            source, pool_ref.at[:, pl.ds(stretch_at * rows, source.shape[1]), :], sems.at[number]
        )

    always = [copy(two_ref, 1, 0), copy(own_ref, REACH, 1), copy(columns_ref, REACH + 1, 2)]
    on_odd = [copy(halfway_ref, 2, 3), copy(swapped_ref, 0, 4)]
    on_even = [copy(swapped_ref, 2, 3), copy(onward_ref, 0, 4)]

    @pl.when(odd == 1)
    def _():
        for item in on_odd:
            item.start()

    @pl.when(odd == 0)
    def _():
        for item in on_even:
            item.start()

    for item in always:
        item.start()
    for item in always + on_odd:
        item.wait()
    dead_at = (REACH + 1) * rows + columns_ref.shape[1]
    for local in range(blocks):
        first_key = pool_ref[0, pl.ds(REACH * rows + local * BLK, 1), :]
        at = pl.ds(dead_at + local * BLK, BLK)
        pool_ref[0, at, :] = jnp.broadcast_to(first_key, (BLK, HD))
        pool_ref[1, at, :] = jnp.zeros((BLK, HD), jnp.bfloat16)


def make_pool(blocks, own, swapped, two_back, halfway, onward, columns):
    rows = (REACH + 2) * blocks * BLK + columns.shape[1]
    return pl.pallas_call(
        functools.partial(pool_kernel, blocks),
        out_shape=jax.ShapeDtypeStruct((2, rows, HD), jnp.bfloat16),
        in_specs=[ANYWHERE] * 6,
        out_specs=IN_VMEM,
        scratch_shapes=[pltpu.SemaphoreType.DMA((5,))],
        compiler_params=SMALL,
        cost_estimate=small_cost(2**22),
    )(own, swapped, two_back, halfway, onward, columns)


def attend_kernel(offsets, blocks, slots_ref, pool_ref, query_ref, *refs):
    number = len(offsets)
    outs, (live_buf, scores_buf, weights_buf) = refs[-3 - number : -3], refs[-3:]
    count = slots_ref.shape[0] // blocks
    alive_slots = pool_ref.shape[1] // BLK - blocks
    columns = PAIR * BLK
    pairs = query_ref.shape[1] // (PAIR * HD)
    live_buf[0] = jnp.zeros((ONES, BLK), jnp.bfloat16)
    live_buf[1] = jnp.ones((ONES, BLK), jnp.bfloat16)
    rank_kvh = lax.axis_index("kvh")

    def head_columns(pair, h):
        return pl.ds(pl.multiple_of((pair * PAIR + h) * HD, HD), HD)

    def products(local, slots, pair, buf):
        rows = pl.ds(pl.multiple_of(local * BLK, BLK), BLK)
        queries = jnp.concatenate([query_ref[rows, head_columns(pair, h)].T for h in range(PAIR)], axis=1)
        keys = jnp.concatenate([pool_ref[0, rows, :] for rows in slots], axis=0)
        scores = jnp.dot(keys, queries, preferred_element_type=jnp.float32)
        key_at = lax.broadcasted_iota(jnp.int32, (BLK, columns), 0)
        query_at = lax.rem(lax.broadcasted_iota(jnp.int32, (BLK, columns), 1), BLK)
        own = jnp.where(key_at <= query_at, scores[:BLK], FAR)
        scores_buf[buf, pl.ds(0, BLK), :] = own
        scores_buf[buf, pl.ds(BLK, (count - 1) * BLK), :] = scores[BLK:]
        best = jnp.maximum(jnp.max(own, axis=0, keepdims=True), jnp.max(scores[BLK:], axis=0, keepdims=True))
        return best

    def soften(buf, best):
        for c in range(count):
            rows = pl.ds(c * BLK, BLK)
            weights = jnp.exp2((scores_buf[buf, rows, :] - best) * EXP2_SCALE)
            weights_buf[buf, rows, :] = weights.astype(jnp.bfloat16)

    def finish(at, slots, live, pair, buf):
        values = jnp.concatenate([pool_ref[1, rows, :] for rows in slots], axis=1)
        left = jnp.concatenate([values, jnp.concatenate([live_buf[n] for n in live], axis=1)], axis=0)
        total = jnp.dot(left, weights_buf[buf], preferred_element_type=jnp.float32)
        result = total[:HD] / total[HD : HD + 1]
        for h in range(PAIR):
            outs[at][:, head_columns(pair, h)] = result[:, h * BLK : (h + 1) * BLK].T.astype(jnp.bfloat16)

    for at, offset in enumerate(offsets):
        local = lax.rem(rank_kvh + offset, blocks)
        places = [slots_ref[local * count + c] for c in range(count)]
        slots = [pl.ds(pl.multiple_of(place * BLK, BLK), BLK) for place in places]
        live = [jnp.where(place < alive_slots, 1, 0) for place in places]

        def two(step, _, at=at, local=local, slots=slots, live=live):
            pair = 2 * step
            best = products(local, slots, pair, 0)
            best_next = products(local, slots, pair + 1, 1)
            soften(0, best)
            finish(at, slots, live, pair, 0)
            soften(1, best_next)
            finish(at, slots, live, pair + 1, 1)
            return 0

        if pairs > 1:
            lax.fori_loop(0, pairs // 2, two, 0)
        else:
            soften(0, products(local, slots, 0, 0))
            finish(at, slots, live, 0, 0)


def attend_call(offsets, blocks, slots, pool, query, after):
    count = slots.shape[0] // blocks
    width = count * BLK
    columns = PAIR * BLK
    query_width = query.shape[1]
    number = len(offsets)
    return pl.pallas_call(
        functools.partial(attend_kernel, offsets, blocks),
        out_shape=[jax.ShapeDtypeStruct((BLK, query_width), jnp.bfloat16)] * number,
        in_specs=[SCALARS, IN_VMEM, IN_VMEM] + [ANYWHERE] * len(after),
        out_specs=[IN_VMEM] * number,
        scratch_shapes=[
            pltpu.VMEM((2, ONES, BLK), jnp.bfloat16),
            pltpu.VMEM((2, width, columns), jnp.float32),
            pltpu.VMEM((2, width, columns), jnp.bfloat16),
        ],
        compiler_params=LIMITS,
        cost_estimate=pl.CostEstimate(
            flops=4 * number * BLK * query_width * width,
            bytes_accessed=number * 2**20,
            transcendentals=number * BLK * query_width // HD * width,
        ),
    )(slots, pool, query, *after)


def assemble_kernel(offsets, *refs):
    pieces, out_ref, sems = refs[:-2], refs[-2], refs[-1]
    count = len(offsets)
    width = pieces[0].shape[1]
    copies = []
    for n, offset in enumerate(offsets):
        source = lax.rem(lax.axis_index("kvh") + count - offset, count)
        at = pl.multiple_of(source * width, width)
        copies.append(pltpu.make_async_copy(pieces[n], out_ref.at[:, pl.ds(at, width)], sems.at[n]))
        copies[-1].start()
    for copy in copies:
        copy.wait()


def assemble(offsets, pieces):
    rows, width = pieces[0].shape
    return pl.pallas_call(
        functools.partial(assemble_kernel, offsets),
        out_shape=jax.ShapeDtypeStruct((rows, width * len(pieces)), jnp.bfloat16),
        in_specs=[IN_VMEM] * len(pieces),
        out_specs=ANYWHERE,
        scratch_shapes=[pltpu.SemaphoreType.DMA((len(pieces),))],
        compiler_params=SMALL,
        cost_estimate=small_cost(2**23),
    )(*pieces)


def window_routes(stretches):
    chips = stretches // 2
    first, mixed, last = [], [], []
    for chip in range(chips):
        y, x = divmod(chip, 4)
        for core in range(2):
            first.append((2 * chip + core, (2 * chip + core + 2) % stretches))
        mixed.append((2 * chip, 2 * chip + 1))
        half_y = y + 1 if x == 2 else y
        half = (half_y * 4 + (x - 1) % 4) % chips
        target = (chip + 2) % chips
        mixed.append((2 * chip + 1, 2 * half))
        last.append((2 * half, 2 * target))
    return first, mixed, last


def exchange(parts, groups):
    return lax.all_to_all(parts, "ctx", split_axis=0, concat_axis=0, axis_index_groups=groups, tiled=True)


def add_up(parts):
    return jnp.sum(parts.astype(jnp.float32), axis=0).astype(jnp.bfloat16)


def spread(part, copies):
    return jnp.broadcast_to(part[None], (copies,) + part.shape)


def shards(query_states, key_states, value_states, verticals, slashes):
    blocks = key_states.shape[0] // BLK
    stretches = lax.axis_size("ctx")
    planes = lax.axis_size("kvh")
    key_value, picked = prepare(verticals, key_states, value_states)

    lines = stretches // ROW
    rows = [[y * ROW + g for g in range(ROW)] for y in range(lines)]
    columns_of = [[y * ROW + g for y in range(lines)] for g in range(ROW)]
    share = add_up(exchange(picked.reshape(ROW, -1, HD), rows))

    share, key_value = lax.optimization_barrier((share, key_value))
    first, mixed, last = window_routes(stretches)
    two_back = lax.ppermute(key_value, "ctx", first)
    halfway = lax.ppermute(key_value, "ctx", mixed)
    swapped = lax.ppermute(two_back, "ctx", [(s, s ^ 1) for s in range(stretches)])
    onward = lax.ppermute(halfway, "ctx", last)

    share = add_up(exchange(spread(share, lines), columns_of))
    columns = exchange(spread(share, ROW), rows).reshape(2, -1, HD)

    slots = plan(blocks, verticals, slashes)
    pool = make_pool(blocks, key_value, swapped, two_back, halfway, onward, columns)
    pieces = []
    came = []
    after = []
    for number, offsets in enumerate(CALLS):
        wanted = tuple(offset % planes for offset in offsets)
        after = after + [pieces[n] for n in ARRIVED.get(number, ())]
        results = attend_call(wanted, blocks, slots, pool, query_states, after)
        after = [results[0]]
        for offset, result in zip(wanted, results):
            if offset:
                result = lax.ppermute(result, "kvh", [(s, (s + offset) % planes) for s in range(planes)])
            pieces.append(result)
            came.append(offset)
    return assemble(tuple(came), pieces)


def solution(mesh):
    return jax.shard_map(
        shards,
        mesh=mesh,
        in_specs=(
            P("ctx", "kvh"),
            P("ctx", "kvh"),
            P("ctx", "kvh"),
            P("kvh", None),
            P("kvh", None),
        ),
        out_specs=P(("ctx", "kvh"), None),
        check_vma=False,
    )
```

```python
import functools

import jax
import jax.numpy as jnp
from jax import lax
from jax.experimental import pallas as pl
from jax.experimental.pallas import tpu as pltpu
from jax.sharding import PartitionSpec as P

HD = 128
BLK = 128
REACH = 3
ONES = 16
FAR = -1e30
EXP2_SCALE = HD ** (-0.5) * 1.4426950408889634
VMEM_BYTES = 32 * 2**20
PAIR = 4
FAR_SIDE = 4
BY_STEPS = -2
OFFSETS = (3, -3, 2, 1, -1, 0)
HALF = BLK // 2

ROW = 8

ANYWHERE = pl.BlockSpec(memory_space=pl.ANY)
SCALARS = pl.BlockSpec(memory_space=pltpu.SMEM)
IN_VMEM = pl.BlockSpec(memory_space=pltpu.VMEM)
LIMITS = pltpu.CompilerParams(vmem_limit_bytes=VMEM_BYTES)
SMALL = pltpu.CompilerParams(vmem_limit_bytes=8 * 2**20)
MOST_VMEM = pltpu.CompilerParams(vmem_limit_bytes=60 * 2**20)


def small_cost(bytes_accessed):
    return pl.CostEstimate(flops=0, bytes_accessed=bytes_accessed, transcendentals=0)


def prepare_kernel(verticals_ref, keys_ref, values_ref, stacked_ref, picked_ref, verticals_buf, values_buf, sems):
    verticals_in = pltpu.make_async_copy(verticals_ref, verticals_buf, sems.at[0])
    values_in = pltpu.make_async_copy(values_ref, values_buf, sems.at[1])
    keys_in = pltpu.make_async_copy(keys_ref, stacked_ref.at[0], sems.at[2])
    values_in.start()
    keys_in.start()
    verticals_in.start()
    blocks = keys_ref.shape[0] // BLK
    values_in.wait()
    for j in range(blocks):
        rows = pl.ds(j * BLK, BLK)
        stacked_ref[1, rows, :] = values_buf[rows, :].T
    keys_in.wait()
    verticals_in.wait()
    for v in range(verticals_ref.shape[1]):
        block = verticals_buf[0, v]
        mine = lax.div(block, blocks) == lax.axis_index("ctx")
        row = pl.multiple_of(lax.rem(block, blocks) * BLK, BLK)
        rows = pl.ds(v * BLK, BLK)

        @pl.when(mine)
        def _(row=row, rows=rows):
            picked_ref[:, rows, :] = stacked_ref[:, pl.ds(row, BLK), :]

        @pl.when(jnp.logical_not(mine))
        def _(rows=rows):
            picked_ref[:, rows, :] = jnp.zeros((2, BLK, HD), jnp.bfloat16)


def prepare(verticals, keys, values):
    stretch = keys.shape[0]
    return pl.pallas_call(
        prepare_kernel,
        out_shape=[
            jax.ShapeDtypeStruct((2, stretch, HD), jnp.bfloat16),
            jax.ShapeDtypeStruct((2, verticals.shape[1] * BLK, HD), jnp.bfloat16),
        ],
        in_specs=[ANYWHERE] * 3,
        out_specs=[IN_VMEM, IN_VMEM],
        scratch_shapes=[
            pltpu.SMEM(verticals.shape, jnp.int32),
            pltpu.VMEM((stretch, HD), jnp.bfloat16),
            pltpu.SemaphoreType.DMA((3,)),
        ],
        compiler_params=MOST_VMEM,
        cost_estimate=small_cost(2**20),
    )(verticals, keys, values)


def plan_kernel(blocks, verticals_ref, slashes_ref, slots_ref):
    slash_count = slashes_ref.shape[1]
    vert_count = verticals_ref.shape[1]
    count = 1 + slash_count + vert_count
    rank_ctx = lax.axis_index("ctx")

    def one(local, _):
        block_now = rank_ctx * blocks + local
        ids = [block_now]
        ids += [block_now - slashes_ref[0, k] for k in range(slash_count)]
        ids += [verticals_ref[0, k] for k in range(vert_count)]
        base = REACH * blocks
        slots = [base + local]
        slots += [base + local - slashes_ref[0, k] for k in range(slash_count)]
        slots += [base + blocks + k for k in range(vert_count)]
        dead = base + blocks + vert_count + local
        slots_ref[local * count] = slots[0]
        for c in range(1, count):
            alive = (ids[c] >= 0) & (ids[c] <= block_now)
            for earlier in range(c):
                alive = alive & (ids[c] != ids[earlier])
            slots_ref[local * count + c] = jnp.where(alive, slots[c], dead)
        return 0

    lax.fori_loop(0, blocks, one, 0)


def plan(blocks, verticals, slashes):
    count = 1 + slashes.shape[1] + verticals.shape[1]
    return pl.pallas_call(
        functools.partial(plan_kernel, blocks),
        out_shape=jax.ShapeDtypeStruct((blocks * count,), jnp.int32),
        in_specs=[SCALARS] * 2,
        out_specs=SCALARS,
        compiler_params=SMALL,
        cost_estimate=small_cost(2**20),
    )(verticals, slashes)


def pool_kernel(blocks, own_ref, swapped_ref, two_ref, halfway_ref, onward_ref, columns_ref, pool_ref, sems):
    odd = lax.rem(lax.axis_index("ctx"), 2)
    rows = blocks * BLK

    def copy(source, stretch_at, number):
        return pltpu.make_async_copy(
            source, pool_ref.at[:, pl.ds(stretch_at * rows, source.shape[1]), :], sems.at[number]
        )

    always = [copy(two_ref, 1, 0), copy(own_ref, REACH, 1), copy(columns_ref, REACH + 1, 2)]
    on_odd = [copy(halfway_ref, 2, 3), copy(swapped_ref, 0, 4)]
    on_even = [copy(swapped_ref, 2, 3), copy(onward_ref, 0, 4)]

    @pl.when(odd == 1)
    def _():
        for item in on_odd:
            item.start()

    @pl.when(odd == 0)
    def _():
        for item in on_even:
            item.start()

    for item in always:
        item.start()
    for item in always + on_odd:
        item.wait()
    dead_at = (REACH + 1) * rows + columns_ref.shape[1]
    for local in range(blocks):
        first_key = pool_ref[0, pl.ds(REACH * rows + local * BLK, 1), :]
        at = pl.ds(dead_at + local * BLK, BLK)
        pool_ref[0, at, :] = jnp.broadcast_to(first_key, (BLK, HD))
        pool_ref[1, at, :] = jnp.zeros((BLK, HD), jnp.bfloat16)


def make_pool(blocks, own, swapped, two_back, halfway, onward, columns):
    rows = (REACH + 2) * blocks * BLK + columns.shape[1]
    return pl.pallas_call(
        functools.partial(pool_kernel, blocks),
        out_shape=jax.ShapeDtypeStruct((2, rows, HD), jnp.bfloat16),
        in_specs=[ANYWHERE] * 6,
        out_specs=IN_VMEM,
        scratch_shapes=[pltpu.SemaphoreType.DMA((5,))],
        compiler_params=SMALL,
        cost_estimate=small_cost(2**22),
    )(own, swapped, two_back, halfway, onward, columns)


def attend_kernel(offsets, blocks, slots_ref, pool_ref, query_ref, *refs):
    number = len(offsets)
    outs, (live_buf, scores_buf, weights_buf) = refs[-3 - number : -3], refs[-3:]
    count = slots_ref.shape[0] // blocks
    alive_slots = pool_ref.shape[1] // BLK - blocks
    columns = PAIR * BLK
    sets = query_ref.shape[1] // (PAIR * HD)
    live_buf[0] = jnp.zeros((ONES, BLK), jnp.bfloat16)
    live_buf[1] = jnp.ones((ONES, BLK), jnp.bfloat16)
    rank_kvh = lax.axis_index("kvh")

    def head_columns(which, h):
        return pl.ds((which * PAIR + h) * HD, HD)

    def products(local, slots, which, buf):
        rows = pl.ds(pl.multiple_of(local * BLK, BLK), BLK)
        queries = jnp.concatenate([query_ref[rows, head_columns(which, h)].T for h in range(PAIR)], axis=1)
        keys = jnp.concatenate([pool_ref[0, rows, :] for rows in slots], axis=0)
        scores = jnp.dot(keys, queries, preferred_element_type=jnp.float32)
        key_at = lax.broadcasted_iota(jnp.int32, (BLK, columns), 0)
        query_at = lax.rem(lax.broadcasted_iota(jnp.int32, (BLK, columns), 1), BLK)
        own = jnp.where(key_at <= query_at, scores[:BLK], FAR)
        scores_buf[buf, pl.ds(0, BLK), :] = own
        scores_buf[buf, pl.ds(BLK, (count - 1) * BLK), :] = scores[BLK:]
        return jnp.maximum(jnp.max(own, axis=0, keepdims=True), jnp.max(scores[BLK:], axis=0, keepdims=True))

    def soften(buf, best):
        for c in range(count):
            rows = pl.ds(c * BLK, BLK)
            weights = jnp.exp2((scores_buf[buf, rows, :] - best) * EXP2_SCALE)
            weights_buf[buf, rows, :] = weights.astype(jnp.bfloat16)

    def store(at, which, h, result):
        where = head_columns(which, h)
        if number == 1:
            outs[0][:, where] = result
        elif at == 0:
            outs[0][:, where] = result[:HALF]
            outs[1][pl.ds(BLK, HALF), where] = result[HALF:]
        else:
            outs[1][pl.ds(0, BLK), where] = result

    def finish(at, slots, live, which, buf):
        values = jnp.concatenate([pool_ref[1, rows, :] for rows in slots], axis=1)
        left = jnp.concatenate([values, jnp.concatenate([live_buf[n] for n in live], axis=1)], axis=0)
        total = jnp.dot(left, weights_buf[buf], preferred_element_type=jnp.float32)
        result = total[:HD] / total[HD : HD + 1]
        for h in range(PAIR):
            store(at, which, h, result[:, h * BLK : (h + 1) * BLK].T.astype(jnp.bfloat16))

    for at, offset in enumerate(offsets):
        local = lax.rem(rank_kvh + offset, blocks)
        places = [slots_ref[local * count + c] for c in range(count)]
        slots = [pl.ds(pl.multiple_of(place * BLK, BLK), BLK) for place in places]
        live = [jnp.where(place < alive_slots, 1, 0) for place in places]
        best = [products(local, slots, which, which % 2) for which in range(min(2, sets))]
        for which in range(sets):
            soften(which % 2, best[which])
            finish(at, slots, live, which, which % 2)
            if which + 2 < sets:
                best.append(products(local, slots, which + 2, which % 2))


def attend_call(offsets, blocks, slots, pool, query, after):
    count = slots.shape[0] // blocks
    width = count * BLK
    columns = PAIR * BLK
    query_width = query.shape[1]
    number = len(offsets)
    rows = (BLK,) if number == 1 else (HALF, BLK + HALF)
    return pl.pallas_call(
        functools.partial(attend_kernel, offsets, blocks),
        out_shape=[jax.ShapeDtypeStruct((n, query_width), jnp.bfloat16) for n in rows],
        in_specs=[SCALARS, IN_VMEM, IN_VMEM] + [ANYWHERE] * len(after),
        out_specs=[IN_VMEM] * number,
        scratch_shapes=[
            pltpu.VMEM((2, ONES, BLK), jnp.bfloat16),
            pltpu.VMEM((2, width, columns), jnp.float32),
            pltpu.VMEM((2, width, columns), jnp.bfloat16),
        ],
        compiler_params=LIMITS,
        cost_estimate=pl.CostEstimate(
            flops=4 * number * BLK * query_width * width,
            bytes_accessed=number * 2**20,
            transcendentals=number * BLK * query_width // HD * width,
        ),
    )(slots, pool, query, *after)


def assemble_kernel(places, planes, *refs):
    pieces, out_ref, sems = refs[:-2], refs[-2], refs[-1]
    width = pieces[0].shape[1]
    copies = []
    for n, (offset, row, rows) in enumerate(places):
        source = lax.rem(lax.axis_index("kvh") + planes - offset, planes)
        at = pl.multiple_of(source * width, width)
        target = out_ref.at[pl.ds(row, rows), pl.ds(at, width)]
        copies.append(pltpu.make_async_copy(pieces[n].at[pl.ds(0, rows), :], target, sems.at[n]))
        copies[-1].start()
    for copy in copies:
        copy.wait()


def assemble(places, planes, pieces):
    width = pieces[0].shape[1]
    return pl.pallas_call(
        functools.partial(assemble_kernel, places, planes),
        out_shape=jax.ShapeDtypeStruct((BLK, width * planes), jnp.bfloat16),
        in_specs=[IN_VMEM] * len(pieces),
        out_specs=ANYWHERE,
        scratch_shapes=[pltpu.SemaphoreType.DMA((len(pieces),))],
        compiler_params=SMALL,
        cost_estimate=small_cost(2**23),
    )(*pieces)


def window_routes(stretches):
    chips = stretches // 2
    first, mixed, last = [], [], []
    for chip in range(chips):
        y, x = divmod(chip, 4)
        for core in range(2):
            first.append((2 * chip + core, (2 * chip + core + 2) % stretches))
        mixed.append((2 * chip, 2 * chip + 1))
        half_y = y + 1 if x == 2 else y
        half = (half_y * 4 + (x - 1) % 4) % chips
        target = (chip + 2) % chips
        mixed.append((2 * chip + 1, 2 * half))
        last.append((2 * half, 2 * target))
    return first, mixed, last


def exchange(parts, groups):
    return lax.all_to_all(parts, "ctx", split_axis=0, concat_axis=0, axis_index_groups=groups, tiled=True)


def add_up(parts):
    return jnp.sum(parts.astype(jnp.float32), axis=0).astype(jnp.bfloat16)


def spread(part, copies):
    return jnp.broadcast_to(part[None], (copies,) + part.shape)


def shards(query_states, key_states, value_states, verticals, slashes):
    blocks = key_states.shape[0] // BLK
    stretches = lax.axis_size("ctx")
    planes = lax.axis_size("kvh")
    key_value, picked = prepare(verticals, key_states, value_states)

    lines = stretches // ROW
    rows = [[y * ROW + g for g in range(ROW)] for y in range(lines)]
    columns_of = [[y * ROW + g for y in range(lines)] for g in range(ROW)]
    share = add_up(exchange(picked.reshape(ROW, -1, HD), rows))
    share = add_up(exchange(spread(share, lines), columns_of))
    columns = exchange(spread(share, ROW), rows).reshape(2, -1, HD)

    first, mixed, last = window_routes(stretches)
    two_back = lax.ppermute(key_value, "ctx", first)
    halfway = lax.ppermute(key_value, "ctx", mixed)
    swapped = lax.ppermute(two_back, "ctx", [(s, s ^ 1) for s in range(stretches)])
    onward = lax.ppermute(halfway, "ctx", last)

    slots = plan(blocks, verticals, slashes)
    pool = make_pool(blocks, key_value, swapped, two_back, halfway, onward, columns)

    def attend(offsets, after):
        return attend_call(tuple(n % planes for n in offsets), blocks, slots, pool, query_states, after)

    def send(block, offset):
        return lax.ppermute(block, "kvh", [(s, (s + offset) % planes) for s in range(planes)])

    upper, bundle = attend((FAR_SIDE, BY_STEPS), [])
    after = [upper]
    upper = send(upper, FAR_SIDE)
    bundle = send(bundle, BY_STEPS)
    lower = send(bundle[BLK:], BY_STEPS)
    pieces = [upper, lower, bundle]
    places = [(FAR_SIDE, 0, HALF), (FAR_SIDE, HALF, HALF), (BY_STEPS % planes, 0, BLK)]
    arrived = {3: [bundle], 4: [upper]}
    for number, offset in enumerate(OFFSETS):
        (result,) = attend((offset,), after + arrived.get(number, []))
        after = [result]
        if offset:
            result = send(result, offset)
        if number == 0:
            arrived[5] = [result]
        pieces.append(result)
        places.append((offset % planes, 0, BLK))
    return assemble(tuple(places), planes, pieces)


def solution(mesh):
    return jax.shard_map(
        shards,
        mesh=mesh,
        in_specs=(
            P("ctx", "kvh"),
            P("ctx", "kvh"),
            P("ctx", "kvh"),
            P("kvh", None),
            P("kvh", None),
        ),
        out_specs=P(("ctx", "kvh"), None),
        check_vma=False,
    )
```

```python
import functools

import jax
import jax.numpy as jnp
from jax import lax
from jax.experimental import pallas as pl
from jax.experimental.pallas import tpu as pltpu
from jax.sharding import PartitionSpec as P

HD = 128
BLK = 128
REACH = 3
ONES = 16
FAR = -1e30
EXP2_SCALE = HD ** (-0.5) * 1.4426950408889634
VMEM_BYTES = 32 * 2**20
PAIR = 4
FAR_SIDE = 4
BY_STEPS = -2
OFFSETS = (3, -3, 2, 1, -1, 0)
HALF = BLK // 2

ROW = 8

ANYWHERE = pl.BlockSpec(memory_space=pl.ANY)
SCALARS = pl.BlockSpec(memory_space=pltpu.SMEM)
IN_VMEM = pl.BlockSpec(memory_space=pltpu.VMEM)
LIMITS = pltpu.CompilerParams(vmem_limit_bytes=VMEM_BYTES)
SMALL = pltpu.CompilerParams(vmem_limit_bytes=8 * 2**20)
MOST_VMEM = pltpu.CompilerParams(vmem_limit_bytes=60 * 2**20)


def small_cost(bytes_accessed):
    return pl.CostEstimate(flops=0, bytes_accessed=bytes_accessed, transcendentals=0)


def prepare_kernel(verticals_ref, keys_ref, values_ref, stacked_ref, picked_ref, verticals_buf, values_buf, sems):
    verticals_in = pltpu.make_async_copy(verticals_ref, verticals_buf, sems.at[0])
    values_in = pltpu.make_async_copy(values_ref, values_buf, sems.at[1])
    keys_in = pltpu.make_async_copy(keys_ref, stacked_ref.at[0], sems.at[2])
    values_in.start()
    keys_in.start()
    verticals_in.start()
    blocks = keys_ref.shape[0] // BLK
    values_in.wait()
    for j in range(blocks):
        rows = pl.ds(j * BLK, BLK)
        stacked_ref[1, rows, :] = values_buf[rows, :].T
    keys_in.wait()
    verticals_in.wait()
    for v in range(verticals_ref.shape[1]):
        block = verticals_buf[0, v]
        mine = lax.div(block, blocks) == lax.axis_index("ctx")
        row = pl.multiple_of(lax.rem(block, blocks) * BLK, BLK)
        rows = pl.ds(v * BLK, BLK)

        @pl.when(mine)
        def _(row=row, rows=rows):
            picked_ref[:, rows, :] = stacked_ref[:, pl.ds(row, BLK), :]

        @pl.when(jnp.logical_not(mine))
        def _(rows=rows):
            picked_ref[:, rows, :] = jnp.zeros((2, BLK, HD), jnp.bfloat16)


def prepare(verticals, keys, values):
    stretch = keys.shape[0]
    return pl.pallas_call(
        prepare_kernel,
        out_shape=[
            jax.ShapeDtypeStruct((2, stretch, HD), jnp.bfloat16),
            jax.ShapeDtypeStruct((2, verticals.shape[1] * BLK, HD), jnp.bfloat16),
        ],
        in_specs=[ANYWHERE] * 3,
        out_specs=[IN_VMEM, IN_VMEM],
        scratch_shapes=[
            pltpu.SMEM(verticals.shape, jnp.int32),
            pltpu.VMEM((stretch, HD), jnp.bfloat16),
            pltpu.SemaphoreType.DMA((3,)),
        ],
        compiler_params=MOST_VMEM,
        cost_estimate=small_cost(2**20),
    )(verticals, keys, values)


def plan_kernel(blocks, verticals_ref, slashes_ref, slots_ref):
    slash_count = slashes_ref.shape[1]
    vert_count = verticals_ref.shape[1]
    count = 1 + slash_count + vert_count
    rank_ctx = lax.axis_index("ctx")

    def one(local, _):
        block_now = rank_ctx * blocks + local
        ids = [block_now]
        ids += [block_now - slashes_ref[0, k] for k in range(slash_count)]
        ids += [verticals_ref[0, k] for k in range(vert_count)]
        base = REACH * blocks
        slots = [base + local]
        slots += [base + local - slashes_ref[0, k] for k in range(slash_count)]
        slots += [base + blocks + k for k in range(vert_count)]
        dead = base + blocks + vert_count + local
        slots_ref[local * count] = slots[0]
        for c in range(1, count):
            alive = (ids[c] >= 0) & (ids[c] <= block_now)
            for earlier in range(c):
                alive = alive & (ids[c] != ids[earlier])
            slots_ref[local * count + c] = jnp.where(alive, slots[c], dead)
        return 0

    lax.fori_loop(0, blocks, one, 0)


def plan(blocks, verticals, slashes):
    count = 1 + slashes.shape[1] + verticals.shape[1]
    return pl.pallas_call(
        functools.partial(plan_kernel, blocks),
        out_shape=jax.ShapeDtypeStruct((blocks * count,), jnp.int32),
        in_specs=[SCALARS] * 2,
        out_specs=SCALARS,
        compiler_params=SMALL,
        cost_estimate=small_cost(2**20),
    )(verticals, slashes)


def pool_kernel(blocks, own_ref, swapped_ref, two_ref, halfway_ref, onward_ref, columns_ref, _, pool_ref, sems):
    odd = lax.rem(lax.axis_index("ctx"), 2)
    rows = blocks * BLK

    def copy(source, stretch_at, number):
        return pltpu.make_async_copy(
            source, pool_ref.at[:, pl.ds(stretch_at * rows, source.shape[1]), :], sems.at[number]
        )

    always = [copy(two_ref, 1, 0), copy(own_ref, REACH, 1), copy(columns_ref, REACH + 1, 2)]
    on_odd = [copy(halfway_ref, 2, 3), copy(swapped_ref, 0, 4)]
    on_even = [copy(swapped_ref, 2, 3), copy(onward_ref, 0, 4)]

    @pl.when(odd == 1)
    def _():
        for item in on_odd:
            item.start()

    @pl.when(odd == 0)
    def _():
        for item in on_even:
            item.start()

    for item in always:
        item.start()
    for item in always + on_odd:
        item.wait()
    dead_at = (REACH + 1) * rows + columns_ref.shape[1]
    for local in range(blocks):
        first_key = pool_ref[0, pl.ds(REACH * rows + local * BLK, 1), :]
        at = pl.ds(dead_at + local * BLK, BLK)
        pool_ref[0, at, :] = jnp.broadcast_to(first_key, (BLK, HD))
        pool_ref[1, at, :] = jnp.zeros((BLK, HD), jnp.bfloat16)


def make_pool(blocks, own, swapped, two_back, halfway, onward, columns, query):
    rows = (REACH + 2) * blocks * BLK + columns.shape[1]
    return pl.pallas_call(
        functools.partial(pool_kernel, blocks),
        out_shape=jax.ShapeDtypeStruct((2, rows, HD), jnp.bfloat16),
        in_specs=[ANYWHERE] * 6 + [IN_VMEM],
        out_specs=IN_VMEM,
        scratch_shapes=[pltpu.SemaphoreType.DMA((5,))],
        compiler_params=SMALL,
        cost_estimate=small_cost(2**22),
    )(own, swapped, two_back, halfway, onward, columns, query)


def attend_kernel(offsets, blocks, slots_ref, pool_ref, query_ref, *refs):
    number = len(offsets)
    outs, (live_buf, scores_buf, weights_buf) = refs[-3 - number : -3], refs[-3:]
    count = slots_ref.shape[0] // blocks
    alive_slots = pool_ref.shape[1] // BLK - blocks
    columns = PAIR * BLK
    sets = query_ref.shape[1] // (PAIR * HD)
    live_buf[0] = jnp.zeros((ONES, BLK), jnp.bfloat16)
    live_buf[1] = jnp.ones((ONES, BLK), jnp.bfloat16)
    rank_kvh = lax.axis_index("kvh")

    def head_columns(which, h):
        return pl.ds((which * PAIR + h) * HD, HD)

    def products(local, slots, which, buf):
        rows = pl.ds(pl.multiple_of(local * BLK, BLK), BLK)
        queries = jnp.concatenate([query_ref[rows, head_columns(which, h)].T for h in range(PAIR)], axis=1)
        keys = jnp.concatenate([pool_ref[0, rows, :] for rows in slots], axis=0)
        scores = jnp.dot(keys, queries, preferred_element_type=jnp.float32)
        key_at = lax.broadcasted_iota(jnp.int32, (BLK, columns), 0)
        query_at = lax.rem(lax.broadcasted_iota(jnp.int32, (BLK, columns), 1), BLK)
        own = jnp.where(key_at <= query_at, scores[:BLK], FAR)
        scores_buf[buf, pl.ds(0, BLK), :] = own
        scores_buf[buf, pl.ds(BLK, (count - 1) * BLK), :] = scores[BLK:]
        return jnp.maximum(jnp.max(own, axis=0, keepdims=True), jnp.max(scores[BLK:], axis=0, keepdims=True))

    def soften(buf, best):
        for c in range(count):
            rows = pl.ds(c * BLK, BLK)
            weights = jnp.exp2((scores_buf[buf, rows, :] - best) * EXP2_SCALE)
            weights_buf[buf, rows, :] = weights.astype(jnp.bfloat16)

    def store(at, which, h, result):
        where = head_columns(which, h)
        if number == 1:
            outs[0][:, where] = result
        elif at == 0:
            outs[0][:, where] = result[:HALF]
            outs[1][pl.ds(BLK, HALF), where] = result[HALF:]
        else:
            outs[1][pl.ds(0, BLK), where] = result

    def finish(at, slots, live, which, buf):
        values = jnp.concatenate([pool_ref[1, rows, :] for rows in slots], axis=1)
        left = jnp.concatenate([values, jnp.concatenate([live_buf[n] for n in live], axis=1)], axis=0)
        total = jnp.dot(left, weights_buf[buf], preferred_element_type=jnp.float32)
        result = total[:HD] / total[HD : HD + 1]
        for h in range(PAIR):
            store(at, which, h, result[:, h * BLK : (h + 1) * BLK].T.astype(jnp.bfloat16))

    for at, offset in enumerate(offsets):
        local = lax.rem(rank_kvh + offset, blocks)
        places = [slots_ref[local * count + c] for c in range(count)]
        slots = [pl.ds(pl.multiple_of(place * BLK, BLK), BLK) for place in places]
        live = [jnp.where(place < alive_slots, 1, 0) for place in places]
        best = [products(local, slots, which, which % 2) for which in range(min(2, sets))]
        for which in range(sets):
            soften(which % 2, best[which])
            finish(at, slots, live, which, which % 2)
            if which + 2 < sets:
                best.append(products(local, slots, which + 2, which % 2))


def attend_call(offsets, blocks, slots, pool, query, after):
    count = slots.shape[0] // blocks
    width = count * BLK
    columns = PAIR * BLK
    query_width = query.shape[1]
    number = len(offsets)
    rows = (BLK,) if number == 1 else (HALF, BLK + HALF)
    return pl.pallas_call(
        functools.partial(attend_kernel, offsets, blocks),
        out_shape=[jax.ShapeDtypeStruct((n, query_width), jnp.bfloat16) for n in rows],
        in_specs=[SCALARS, IN_VMEM, IN_VMEM] + [ANYWHERE] * len(after),
        out_specs=[IN_VMEM] * number,
        scratch_shapes=[
            pltpu.VMEM((2, ONES, BLK), jnp.bfloat16),
            pltpu.VMEM((2, width, columns), jnp.float32),
            pltpu.VMEM((2, width, columns), jnp.bfloat16),
        ],
        compiler_params=LIMITS,
        cost_estimate=pl.CostEstimate(
            flops=4 * number * BLK * query_width * width,
            bytes_accessed=number * 2**20,
            transcendentals=number * BLK * query_width // HD * width,
        ),
    )(slots, pool, query, *after)


def assemble_kernel(places, planes, *refs):
    pieces, out_ref, sems = refs[:-2], refs[-2], refs[-1]
    width = pieces[0].shape[1]
    copies = []
    for n, (offset, row, rows) in enumerate(places):
        source = lax.rem(lax.axis_index("kvh") + planes - offset, planes)
        at = pl.multiple_of(source * width, width)
        target = out_ref.at[pl.ds(row, rows), pl.ds(at, width)]
        copies.append(pltpu.make_async_copy(pieces[n].at[pl.ds(0, rows), :], target, sems.at[n]))
        copies[-1].start()
    for copy in copies:
        copy.wait()


def assemble(places, planes, pieces):
    width = pieces[0].shape[1]
    return pl.pallas_call(
        functools.partial(assemble_kernel, places, planes),
        out_shape=jax.ShapeDtypeStruct((BLK, width * planes), jnp.bfloat16),
        in_specs=[IN_VMEM] * len(pieces),
        out_specs=ANYWHERE,
        scratch_shapes=[pltpu.SemaphoreType.DMA((len(pieces),))],
        compiler_params=SMALL,
        cost_estimate=small_cost(2**23),
    )(*pieces)


def window_routes(stretches):
    chips = stretches // 2
    first, mixed, last = [], [], []
    for chip in range(chips):
        y, x = divmod(chip, 4)
        for core in range(2):
            first.append((2 * chip + core, (2 * chip + core + 2) % stretches))
        mixed.append((2 * chip, 2 * chip + 1))
        half_y = y + 1 if x == 2 else y
        half = (half_y * 4 + (x - 1) % 4) % chips
        target = (chip + 2) % chips
        mixed.append((2 * chip + 1, 2 * half))
        last.append((2 * half, 2 * target))
    return first, mixed, last


def exchange(parts, groups):
    return lax.all_to_all(parts, "ctx", split_axis=0, concat_axis=0, axis_index_groups=groups, tiled=True)


def add_up(parts):
    return jnp.sum(parts.astype(jnp.float32), axis=0).astype(jnp.bfloat16)


def spread(part, copies):
    return jnp.broadcast_to(part[None], (copies,) + part.shape)


def shards(query_states, key_states, value_states, verticals, slashes):
    blocks = key_states.shape[0] // BLK
    stretches = lax.axis_size("ctx")
    planes = lax.axis_size("kvh")
    key_value, picked = prepare(verticals, key_states, value_states)

    lines = stretches // ROW
    rows = [[y * ROW + g for g in range(ROW)] for y in range(lines)]
    columns_of = [[y * ROW + g for y in range(lines)] for g in range(ROW)]
    share = add_up(exchange(picked.reshape(ROW, -1, HD), rows))
    share = add_up(exchange(spread(share, lines), columns_of))

    share, key_value = lax.optimization_barrier((share, key_value))
    first, mixed, last = window_routes(stretches)
    two_back = lax.ppermute(key_value, "ctx", first)
    halfway = lax.ppermute(key_value, "ctx", mixed)
    swapped = lax.ppermute(two_back, "ctx", [(s, s ^ 1) for s in range(stretches)])
    onward = lax.ppermute(halfway, "ctx", last)

    columns = exchange(spread(share, ROW), rows).reshape(2, -1, HD)
    slots = plan(blocks, verticals, slashes)
    pool = make_pool(blocks, key_value, swapped, two_back, halfway, onward, columns, query_states)

    def attend(offsets, after):
        return attend_call(tuple(n % planes for n in offsets), blocks, slots, pool, query_states, after)

    def send(block, offset):
        return lax.ppermute(block, "kvh", [(s, (s + offset) % planes) for s in range(planes)])

    upper, bundle = attend((FAR_SIDE, BY_STEPS), [])
    after = [upper]
    upper = send(upper, FAR_SIDE)
    bundle = send(bundle, BY_STEPS)
    lower = send(bundle[BLK:], BY_STEPS)
    pieces = [upper, lower, bundle]
    places = [(FAR_SIDE, 0, HALF), (FAR_SIDE, HALF, HALF), (BY_STEPS % planes, 0, BLK)]
    arrived = {3: [bundle], 4: [upper]}
    for number, offset in enumerate(OFFSETS):
        (result,) = attend((offset,), after + arrived.get(number, []))
        after = [result]
        if offset:
            result = send(result, offset)
        if number == 0:
            arrived[5] = [result]
        pieces.append(result)
        places.append((offset % planes, 0, BLK))
    return assemble(tuple(places), planes, pieces)


def solution(mesh):
    return jax.shard_map(
        shards,
        mesh=mesh,
        in_specs=(
            P("ctx", "kvh"),
            P("ctx", "kvh"),
            P("ctx", "kvh"),
            P("kvh", None),
            P("kvh", None),
        ),
        out_specs=P(("ctx", "kvh"), None),
        check_vma=False,
    )
```

```python
import functools

import jax
import jax.numpy as jnp
from jax import lax
from jax.experimental import pallas as pl
from jax.experimental.pallas import tpu as pltpu
from jax.sharding import PartitionSpec as P

HD = 128
BLK = 128
REACH = 3
ONES = 16
FAR = -1e30
EXP2_SCALE = HD ** (-0.5) * 1.4426950408889634
VMEM_BYTES = 32 * 2**20
PAIR = 4
FAR_SIDE = 4
BY_STEPS = -2
OFFSETS = (3, -3, 2, 1, -1, 0)
HALF = BLK // 2

ROW = 8

ANYWHERE = pl.BlockSpec(memory_space=pl.ANY)
SCALARS = pl.BlockSpec(memory_space=pltpu.SMEM)
IN_VMEM = pl.BlockSpec(memory_space=pltpu.VMEM)
LIMITS = pltpu.CompilerParams(vmem_limit_bytes=VMEM_BYTES)
SMALL = pltpu.CompilerParams(vmem_limit_bytes=8 * 2**20)
MOST_VMEM = pltpu.CompilerParams(vmem_limit_bytes=60 * 2**20)


def small_cost(bytes_accessed):
    return pl.CostEstimate(flops=0, bytes_accessed=bytes_accessed, transcendentals=0)


def prepare_kernel(verticals_ref, keys_ref, values_ref, stacked_ref, picked_ref, verticals_buf, values_buf, sems):
    verticals_in = pltpu.make_async_copy(verticals_ref, verticals_buf, sems.at[0])
    values_in = pltpu.make_async_copy(values_ref, values_buf, sems.at[1])
    keys_in = pltpu.make_async_copy(keys_ref, stacked_ref.at[0], sems.at[2])
    values_in.start()
    keys_in.start()
    verticals_in.start()
    blocks = keys_ref.shape[0] // BLK
    values_in.wait()
    for j in range(blocks):
        rows = pl.ds(j * BLK, BLK)
        stacked_ref[1, rows, :] = values_buf[rows, :].T
    keys_in.wait()
    verticals_in.wait()
    for v in range(verticals_ref.shape[1]):
        block = verticals_buf[0, v]
        mine = lax.div(block, blocks) == lax.axis_index("ctx")
        row = pl.multiple_of(lax.rem(block, blocks) * BLK, BLK)
        rows = pl.ds(v * BLK, BLK)

        @pl.when(mine)
        def _(row=row, rows=rows):
            picked_ref[:, rows, :] = stacked_ref[:, pl.ds(row, BLK), :]

        @pl.when(jnp.logical_not(mine))
        def _(rows=rows):
            picked_ref[:, rows, :] = jnp.zeros((2, BLK, HD), jnp.bfloat16)


def prepare(verticals, keys, values):
    stretch = keys.shape[0]
    return pl.pallas_call(
        prepare_kernel,
        out_shape=[
            jax.ShapeDtypeStruct((2, stretch, HD), jnp.bfloat16),
            jax.ShapeDtypeStruct((2, verticals.shape[1] * BLK, HD), jnp.bfloat16),
        ],
        in_specs=[ANYWHERE] * 3,
        out_specs=[IN_VMEM, IN_VMEM],
        scratch_shapes=[
            pltpu.SMEM(verticals.shape, jnp.int32),
            pltpu.VMEM((stretch, HD), jnp.bfloat16),
            pltpu.SemaphoreType.DMA((3,)),
        ],
        compiler_params=MOST_VMEM,
        cost_estimate=small_cost(2**20),
    )(verticals, keys, values)


def plan_kernel(blocks, verticals_ref, slashes_ref, slots_ref):
    slash_count = slashes_ref.shape[1]
    vert_count = verticals_ref.shape[1]
    count = 1 + slash_count + vert_count
    rank_ctx = lax.axis_index("ctx")

    def one(local, _):
        block_now = rank_ctx * blocks + local
        ids = [block_now]
        ids += [block_now - slashes_ref[0, k] for k in range(slash_count)]
        ids += [verticals_ref[0, k] for k in range(vert_count)]
        base = REACH * blocks
        slots = [base + local]
        slots += [base + local - slashes_ref[0, k] for k in range(slash_count)]
        slots += [base + blocks + k for k in range(vert_count)]
        dead = base + blocks + vert_count + local
        slots_ref[local * count] = slots[0]
        for c in range(1, count):
            alive = (ids[c] >= 0) & (ids[c] <= block_now)
            for earlier in range(c):
                alive = alive & (ids[c] != ids[earlier])
            slots_ref[local * count + c] = jnp.where(alive, slots[c], dead)
        return 0

    lax.fori_loop(0, blocks, one, 0)


def plan(blocks, verticals, slashes):
    count = 1 + slashes.shape[1] + verticals.shape[1]
    return pl.pallas_call(
        functools.partial(plan_kernel, blocks),
        out_shape=jax.ShapeDtypeStruct((blocks * count,), jnp.int32),
        in_specs=[SCALARS] * 2,
        out_specs=SCALARS,
        compiler_params=SMALL,
        cost_estimate=small_cost(2**20),
    )(verticals, slashes)


def pool_kernel(blocks, own_ref, swapped_ref, two_ref, halfway_ref, onward_ref, columns_ref, pool_ref, sems):
    odd = lax.rem(lax.axis_index("ctx"), 2)
    rows = blocks * BLK

    def copy(source, stretch_at, number):
        return pltpu.make_async_copy(
            source, pool_ref.at[:, pl.ds(stretch_at * rows, source.shape[1]), :], sems.at[number]
        )

    always = [copy(two_ref, 1, 0), copy(own_ref, REACH, 1), copy(columns_ref, REACH + 1, 2)]
    on_odd = [copy(halfway_ref, 2, 3), copy(swapped_ref, 0, 4)]
    on_even = [copy(swapped_ref, 2, 3), copy(onward_ref, 0, 4)]

    @pl.when(odd == 1)
    def _():
        for item in on_odd:
            item.start()

    @pl.when(odd == 0)
    def _():
        for item in on_even:
            item.start()

    for item in always:
        item.start()
    for item in always + on_odd:
        item.wait()
    dead_at = (REACH + 1) * rows + columns_ref.shape[1]
    for local in range(blocks):
        first_key = pool_ref[0, pl.ds(REACH * rows + local * BLK, 1), :]
        at = pl.ds(dead_at + local * BLK, BLK)
        pool_ref[0, at, :] = jnp.broadcast_to(first_key, (BLK, HD))
        pool_ref[1, at, :] = jnp.zeros((BLK, HD), jnp.bfloat16)


def make_pool(blocks, own, swapped, two_back, halfway, onward, columns):
    rows = (REACH + 2) * blocks * BLK + columns.shape[1]
    return pl.pallas_call(
        functools.partial(pool_kernel, blocks),
        out_shape=jax.ShapeDtypeStruct((2, rows, HD), jnp.bfloat16),
        in_specs=[ANYWHERE] * 6,
        out_specs=IN_VMEM,
        scratch_shapes=[pltpu.SemaphoreType.DMA((5,))],
        compiler_params=SMALL,
        cost_estimate=small_cost(2**22),
    )(own, swapped, two_back, halfway, onward, columns)


def attend_kernel(offsets, blocks, slots_ref, pool_ref, query_ref, *refs):
    number = len(offsets)
    outs, (live_buf, scores_buf, weights_buf) = refs[-3 - number : -3], refs[-3:]
    count = slots_ref.shape[0] // blocks
    alive_slots = pool_ref.shape[1] // BLK - blocks
    columns = PAIR * BLK
    sets = query_ref.shape[1] // (PAIR * HD)
    live_buf[0] = jnp.zeros((ONES, BLK), jnp.bfloat16)
    live_buf[1] = jnp.ones((ONES, BLK), jnp.bfloat16)
    rank_kvh = lax.axis_index("kvh")

    def head_columns(which, h):
        return pl.ds((which * PAIR + h) * HD, HD)

    def products(local, slots, which, buf):
        rows = pl.ds(pl.multiple_of(local * BLK, BLK), BLK)
        queries = jnp.concatenate([query_ref[rows, head_columns(which, h)].T for h in range(PAIR)], axis=1)
        keys = jnp.concatenate([pool_ref[0, rows, :] for rows in slots], axis=0)
        scores = jnp.dot(keys, queries, preferred_element_type=jnp.float32)
        key_at = lax.broadcasted_iota(jnp.int32, (BLK, columns), 0)
        query_at = lax.rem(lax.broadcasted_iota(jnp.int32, (BLK, columns), 1), BLK)
        own = jnp.where(key_at <= query_at, scores[:BLK], FAR)
        scores_buf[buf, pl.ds(0, BLK), :] = own
        scores_buf[buf, pl.ds(BLK, (count - 1) * BLK), :] = scores[BLK:]
        return jnp.maximum(jnp.max(own, axis=0, keepdims=True), jnp.max(scores[BLK:], axis=0, keepdims=True))

    def soften(buf, best):
        for c in range(count):
            rows = pl.ds(c * BLK, BLK)
            weights = jnp.exp2((scores_buf[buf, rows, :] - best) * EXP2_SCALE)
            weights_buf[buf, rows, :] = weights.astype(jnp.bfloat16)

    def store(at, which, h, result):
        where = head_columns(which, h)
        if number == 1:
            outs[0][:, where] = result
        elif at == 0:
            outs[0][:, where] = result[:HALF]
            outs[1][pl.ds(BLK, HALF), where] = result[HALF:]
        else:
            outs[1][pl.ds(0, BLK), where] = result

    def finish(at, slots, live, which, buf):
        values = jnp.concatenate([pool_ref[1, rows, :] for rows in slots], axis=1)
        left = jnp.concatenate([values, jnp.concatenate([live_buf[n] for n in live], axis=1)], axis=0)
        total = jnp.dot(left, weights_buf[buf], preferred_element_type=jnp.float32)
        result = total[:HD] / total[HD : HD + 1]
        for h in range(PAIR):
            store(at, which, h, result[:, h * BLK : (h + 1) * BLK].T.astype(jnp.bfloat16))

    for at, offset in enumerate(offsets):
        local = lax.rem(rank_kvh + offset, blocks)
        places = [slots_ref[local * count + c] for c in range(count)]
        slots = [pl.ds(pl.multiple_of(place * BLK, BLK), BLK) for place in places]
        live = [jnp.where(place < alive_slots, 1, 0) for place in places]
        best = [products(local, slots, which, which % 2) for which in range(min(2, sets))]
        for which in range(sets):
            soften(which % 2, best[which])
            finish(at, slots, live, which, which % 2)
            if which + 2 < sets:
                best.append(products(local, slots, which + 2, which % 2))


def attend_call(offsets, blocks, slots, pool, query, after):
    count = slots.shape[0] // blocks
    width = count * BLK
    columns = PAIR * BLK
    query_width = query.shape[1]
    number = len(offsets)
    rows = (BLK,) if number == 1 else (HALF, BLK + HALF)
    return pl.pallas_call(
        functools.partial(attend_kernel, offsets, blocks),
        out_shape=[jax.ShapeDtypeStruct((n, query_width), jnp.bfloat16) for n in rows],
        in_specs=[SCALARS, IN_VMEM, IN_VMEM] + [ANYWHERE] * len(after),
        out_specs=[IN_VMEM] * number,
        scratch_shapes=[
            pltpu.VMEM((2, ONES, BLK), jnp.bfloat16),
            pltpu.VMEM((2, width, columns), jnp.float32),
            pltpu.VMEM((2, width, columns), jnp.bfloat16),
        ],
        compiler_params=LIMITS,
        cost_estimate=pl.CostEstimate(
            flops=4 * number * BLK * query_width * width,
            bytes_accessed=number * 2**20,
            transcendentals=number * BLK * query_width // HD * width,
        ),
    )(slots, pool, query, *after)


def assemble_kernel(places, planes, *refs):
    pieces, out_ref, sems = refs[:-2], refs[-2], refs[-1]
    width = pieces[0].shape[1]
    copies = []
    for n, (offset, row, rows) in enumerate(places):
        source = lax.rem(lax.axis_index("kvh") + planes - offset, planes)
        at = pl.multiple_of(source * width, width)
        target = out_ref.at[pl.ds(row, rows), pl.ds(at, width)]
        copies.append(pltpu.make_async_copy(pieces[n].at[pl.ds(0, rows), :], target, sems.at[n]))
        copies[-1].start()
    for copy in copies:
        copy.wait()


def assemble(places, planes, pieces):
    width = pieces[0].shape[1]
    return pl.pallas_call(
        functools.partial(assemble_kernel, places, planes),
        out_shape=jax.ShapeDtypeStruct((BLK, width * planes), jnp.bfloat16),
        in_specs=[IN_VMEM] * len(pieces),
        out_specs=ANYWHERE,
        scratch_shapes=[pltpu.SemaphoreType.DMA((len(pieces),))],
        compiler_params=SMALL,
        cost_estimate=small_cost(2**23),
    )(*pieces)


def window_routes(stretches):
    chips = stretches // 2
    first, mixed, last = [], [], []
    for chip in range(chips):
        y, x = divmod(chip, 4)
        for core in range(2):
            first.append((2 * chip + core, (2 * chip + core + 2) % stretches))
        mixed.append((2 * chip, 2 * chip + 1))
        half_y = y + 1 if x == 2 else y
        half = (half_y * 4 + (x - 1) % 4) % chips
        target = (chip + 2) % chips
        mixed.append((2 * chip + 1, 2 * half))
        last.append((2 * half, 2 * target))
    return first, mixed, last


def exchange(parts, groups):
    return lax.all_to_all(parts, "ctx", split_axis=0, concat_axis=0, axis_index_groups=groups, tiled=True)


def add_up(parts):
    return jnp.sum(parts.astype(jnp.float32), axis=0).astype(jnp.bfloat16)


def spread(part, copies):
    return jnp.broadcast_to(part[None], (copies,) + part.shape)


def shards(query_states, key_states, value_states, verticals, slashes):
    blocks = key_states.shape[0] // BLK
    stretches = lax.axis_size("ctx")
    planes = lax.axis_size("kvh")
    key_value, picked = prepare(verticals, key_states, value_states)

    lines = stretches // ROW
    rows = [[y * ROW + g for g in range(ROW)] for y in range(lines)]
    columns_of = [[y * ROW + g for y in range(lines)] for g in range(ROW)]
    share = add_up(exchange(picked.reshape(ROW, -1, HD), rows))
    share = add_up(exchange(spread(share, lines), columns_of))

    first, mixed, last = window_routes(stretches)
    two_back = lax.ppermute(key_value, "ctx", first)
    halfway = lax.ppermute(key_value, "ctx", mixed)
    share, two_back = lax.optimization_barrier((share, two_back))
    swapped = lax.ppermute(two_back, "ctx", [(s, s ^ 1) for s in range(stretches)])
    onward = lax.ppermute(halfway, "ctx", last)

    columns = exchange(spread(share, ROW), rows).reshape(2, -1, HD)
    slots = plan(blocks, verticals, slashes)
    pool = make_pool(blocks, key_value, swapped, two_back, halfway, onward, columns)

    def attend(offsets, after):
        return attend_call(tuple(n % planes for n in offsets), blocks, slots, pool, query_states, after)

    def send(block, offset):
        return lax.ppermute(block, "kvh", [(s, (s + offset) % planes) for s in range(planes)])

    upper, bundle = attend((FAR_SIDE, BY_STEPS), [])
    after = [upper]
    upper = send(upper, FAR_SIDE)
    bundle = send(bundle, BY_STEPS)
    lower = send(bundle[BLK:], BY_STEPS)
    pieces = [upper, lower, bundle]
    places = [(FAR_SIDE, 0, HALF), (FAR_SIDE, HALF, HALF), (BY_STEPS % planes, 0, BLK)]
    arrived = {3: [bundle], 4: [upper, lower]}
    for number, offset in enumerate(OFFSETS):
        (result,) = attend((offset,), after + arrived.get(number, []))
        after = [result]
        if offset:
            result = send(result, offset)
        if number == 0:
            arrived[5] = [result]
        pieces.append(result)
        places.append((offset % planes, 0, BLK))
    return assemble(tuple(places), planes, pieces)


def solution(mesh):
    return jax.shard_map(
        shards,
        mesh=mesh,
        in_specs=(
            P("ctx", "kvh"),
            P("ctx", "kvh"),
            P("ctx", "kvh"),
            P("kvh", None),
            P("kvh", None),
        ),
        out_specs=P(("ctx", "kvh"), None),
        check_vma=False,
    )
```

```python
import functools

import jax
import jax.numpy as jnp
from jax import lax
from jax.experimental import pallas as pl
from jax.experimental.pallas import tpu as pltpu
from jax.sharding import PartitionSpec as P

HD = 128
BLK = 128
REACH = 3
ONES = 16
FAR = -1e30
EXP2_SCALE = HD ** (-0.5) * 1.4426950408889634
VMEM_BYTES = 32 * 2**20
PAIR = 4
FAR_SIDE = 4
BY_STEPS = -2
OFFSETS = (3, -3, 2, 1, -1, 0)
HALF = BLK // 2

ROW = 8

ANYWHERE = pl.BlockSpec(memory_space=pl.ANY)
SCALARS = pl.BlockSpec(memory_space=pltpu.SMEM)
IN_VMEM = pl.BlockSpec(memory_space=pltpu.VMEM)
LIMITS = pltpu.CompilerParams(vmem_limit_bytes=VMEM_BYTES)
SMALL = pltpu.CompilerParams(vmem_limit_bytes=8 * 2**20)
MOST_VMEM = pltpu.CompilerParams(vmem_limit_bytes=60 * 2**20)


def small_cost(bytes_accessed):
    return pl.CostEstimate(flops=0, bytes_accessed=bytes_accessed, transcendentals=0)


def prepare_kernel(verticals_ref, keys_ref, values_ref, stacked_ref, picked_ref, verticals_buf, values_buf, sems):
    verticals_in = pltpu.make_async_copy(verticals_ref, verticals_buf, sems.at[0])
    values_in = pltpu.make_async_copy(values_ref, values_buf, sems.at[1])
    keys_in = pltpu.make_async_copy(keys_ref, stacked_ref.at[0], sems.at[2])
    values_in.start()
    keys_in.start()
    verticals_in.start()
    blocks = keys_ref.shape[0] // BLK
    values_in.wait()
    for j in range(blocks):
        rows = pl.ds(j * BLK, BLK)
        stacked_ref[1, rows, :] = values_buf[rows, :].T
    keys_in.wait()
    verticals_in.wait()
    for v in range(verticals_ref.shape[1]):
        block = verticals_buf[0, v]
        mine = lax.div(block, blocks) == lax.axis_index("ctx")
        row = pl.multiple_of(lax.rem(block, blocks) * BLK, BLK)
        rows = pl.ds(v * BLK, BLK)

        @pl.when(mine)
        def _(row=row, rows=rows):
            picked_ref[:, rows, :] = stacked_ref[:, pl.ds(row, BLK), :]

        @pl.when(jnp.logical_not(mine))
        def _(rows=rows):
            picked_ref[:, rows, :] = jnp.zeros((2, BLK, HD), jnp.bfloat16)


def prepare(verticals, keys, values):
    stretch = keys.shape[0]
    return pl.pallas_call(
        prepare_kernel,
        out_shape=[
            jax.ShapeDtypeStruct((2, stretch, HD), jnp.bfloat16),
            jax.ShapeDtypeStruct((2, verticals.shape[1] * BLK, HD), jnp.bfloat16),
        ],
        in_specs=[ANYWHERE] * 3,
        out_specs=[IN_VMEM, IN_VMEM],
        scratch_shapes=[
            pltpu.SMEM(verticals.shape, jnp.int32),
            pltpu.VMEM((stretch, HD), jnp.bfloat16),
            pltpu.SemaphoreType.DMA((3,)),
        ],
        compiler_params=MOST_VMEM,
        cost_estimate=small_cost(2**20),
    )(verticals, keys, values)


def plan_kernel(blocks, verticals_ref, slashes_ref, slots_ref):
    slash_count = slashes_ref.shape[1]
    vert_count = verticals_ref.shape[1]
    count = 1 + slash_count + vert_count
    rank_ctx = lax.axis_index("ctx")

    def one(local, _):
        block_now = rank_ctx * blocks + local
        ids = [block_now]
        ids += [block_now - slashes_ref[0, k] for k in range(slash_count)]
        ids += [verticals_ref[0, k] for k in range(vert_count)]
        base = REACH * blocks
        slots = [base + local]
        slots += [base + local - slashes_ref[0, k] for k in range(slash_count)]
        slots += [base + blocks + k for k in range(vert_count)]
        dead = base + blocks + vert_count + local
        slots_ref[local * count] = slots[0]
        for c in range(1, count):
            alive = (ids[c] >= 0) & (ids[c] <= block_now)
            for earlier in range(c):
                alive = alive & (ids[c] != ids[earlier])
            slots_ref[local * count + c] = jnp.where(alive, slots[c], dead)
        return 0

    lax.fori_loop(0, blocks, one, 0)


def plan(blocks, verticals, slashes):
    count = 1 + slashes.shape[1] + verticals.shape[1]
    return pl.pallas_call(
        functools.partial(plan_kernel, blocks),
        out_shape=jax.ShapeDtypeStruct((blocks * count,), jnp.int32),
        in_specs=[SCALARS] * 2,
        out_specs=SCALARS,
        compiler_params=SMALL,
        cost_estimate=small_cost(2**20),
    )(verticals, slashes)


def pool_kernel(blocks, own_ref, swapped_ref, two_ref, halfway_ref, onward_ref, columns_ref, pool_ref, sems):
    odd = lax.rem(lax.axis_index("ctx"), 2)
    rows = blocks * BLK

    def copy(source, stretch_at, number):
        return pltpu.make_async_copy(
            source, pool_ref.at[:, pl.ds(stretch_at * rows, source.shape[1]), :], sems.at[number]
        )

    always = [copy(two_ref, 1, 0), copy(own_ref, REACH, 1), copy(columns_ref, REACH + 1, 2)]
    on_odd = [copy(halfway_ref, 2, 3), copy(swapped_ref, 0, 4)]
    on_even = [copy(swapped_ref, 2, 3), copy(onward_ref, 0, 4)]

    @pl.when(odd == 1)
    def _():
        for item in on_odd:
            item.start()

    @pl.when(odd == 0)
    def _():
        for item in on_even:
            item.start()

    for item in always:
        item.start()
    for item in always + on_odd:
        item.wait()
    dead_at = (REACH + 1) * rows + columns_ref.shape[1]
    for local in range(blocks):
        first_key = pool_ref[0, pl.ds(REACH * rows + local * BLK, 1), :]
        at = pl.ds(dead_at + local * BLK, BLK)
        pool_ref[0, at, :] = jnp.broadcast_to(first_key, (BLK, HD))
        pool_ref[1, at, :] = jnp.zeros((BLK, HD), jnp.bfloat16)


def make_pool(blocks, own, swapped, two_back, halfway, onward, columns):
    rows = (REACH + 2) * blocks * BLK + columns.shape[1]
    return pl.pallas_call(
        functools.partial(pool_kernel, blocks),
        out_shape=jax.ShapeDtypeStruct((2, rows, HD), jnp.bfloat16),
        in_specs=[ANYWHERE] * 6,
        out_specs=IN_VMEM,
        scratch_shapes=[pltpu.SemaphoreType.DMA((5,))],
        compiler_params=SMALL,
        cost_estimate=small_cost(2**22),
    )(own, swapped, two_back, halfway, onward, columns)


def attend_kernel(offsets, blocks, slots_ref, pool_ref, query_ref, *refs):
    number = len(offsets)
    outs, (live_buf, scores_buf, weights_buf) = refs[-3 - number : -3], refs[-3:]
    count = slots_ref.shape[0] // blocks
    alive_slots = pool_ref.shape[1] // BLK - blocks
    columns = PAIR * BLK
    sets = query_ref.shape[1] // (PAIR * HD)
    live_buf[0] = jnp.zeros((ONES, BLK), jnp.bfloat16)
    live_buf[1] = jnp.ones((ONES, BLK), jnp.bfloat16)
    rank_kvh = lax.axis_index("kvh")

    def head_columns(which, h):
        return pl.ds((which * PAIR + h) * HD, HD)

    def products(local, slots, which, buf):
        rows = pl.ds(pl.multiple_of(local * BLK, BLK), BLK)
        queries = jnp.concatenate([query_ref[rows, head_columns(which, h)].T for h in range(PAIR)], axis=1)
        keys = jnp.concatenate([pool_ref[0, rows, :] for rows in slots], axis=0)
        scores = jnp.dot(keys, queries, preferred_element_type=jnp.float32)
        key_at = lax.broadcasted_iota(jnp.int32, (BLK, columns), 0)
        query_at = lax.rem(lax.broadcasted_iota(jnp.int32, (BLK, columns), 1), BLK)
        own = jnp.where(key_at <= query_at, scores[:BLK], FAR)
        scores_buf[buf, pl.ds(0, BLK), :] = own
        scores_buf[buf, pl.ds(BLK, (count - 1) * BLK), :] = scores[BLK:]
        return jnp.maximum(jnp.max(own, axis=0, keepdims=True), jnp.max(scores[BLK:], axis=0, keepdims=True))

    def soften(buf, best):
        for c in range(count):
            rows = pl.ds(c * BLK, BLK)
            weights = jnp.exp2((scores_buf[buf, rows, :] - best) * EXP2_SCALE)
            weights_buf[buf, rows, :] = weights.astype(jnp.bfloat16)

    def store(at, which, h, result):
        where = head_columns(which, h)
        if number == 1:
            outs[0][:, where] = result
        elif at == 0:
            outs[0][:, where] = result[:HALF]
            outs[1][pl.ds(BLK, HALF), where] = result[HALF:]
        else:
            outs[1][pl.ds(0, BLK), where] = result

    def finish(at, slots, live, which, buf):
        values = jnp.concatenate([pool_ref[1, rows, :] for rows in slots], axis=1)
        left = jnp.concatenate([values, jnp.concatenate([live_buf[n] for n in live], axis=1)], axis=0)
        total = jnp.dot(left, weights_buf[buf], preferred_element_type=jnp.float32)
        result = total[:HD] / total[HD : HD + 1]
        for h in range(PAIR):
            store(at, which, h, result[:, h * BLK : (h + 1) * BLK].T.astype(jnp.bfloat16))

    for at, offset in enumerate(offsets):
        local = lax.rem(rank_kvh + offset, blocks)
        places = [slots_ref[local * count + c] for c in range(count)]
        slots = [pl.ds(pl.multiple_of(place * BLK, BLK), BLK) for place in places]
        live = [jnp.where(place < alive_slots, 1, 0) for place in places]
        best = [products(local, slots, which, which % 2) for which in range(min(2, sets))]
        for which in range(sets):
            soften(which % 2, best[which])
            finish(at, slots, live, which, which % 2)
            if which + 2 < sets:
                best.append(products(local, slots, which + 2, which % 2))


def attend_call(offsets, blocks, slots, pool, query, after):
    count = slots.shape[0] // blocks
    width = count * BLK
    columns = PAIR * BLK
    query_width = query.shape[1]
    number = len(offsets)
    rows = (BLK,) if number == 1 else (HALF, BLK + HALF)
    return pl.pallas_call(
        functools.partial(attend_kernel, offsets, blocks),
        out_shape=[jax.ShapeDtypeStruct((n, query_width), jnp.bfloat16) for n in rows],
        in_specs=[SCALARS, IN_VMEM, IN_VMEM] + [ANYWHERE] * len(after),
        out_specs=[IN_VMEM] * number,
        scratch_shapes=[
            pltpu.VMEM((2, ONES, BLK), jnp.bfloat16),
            pltpu.VMEM((2, width, columns), jnp.float32),
            pltpu.VMEM((2, width, columns), jnp.bfloat16),
        ],
        compiler_params=LIMITS,
        cost_estimate=pl.CostEstimate(
            flops=4 * number * BLK * query_width * width,
            bytes_accessed=number * 2**20,
            transcendentals=number * BLK * query_width // HD * width,
        ),
    )(slots, pool, query, *after)


def assemble_kernel(places, planes, *refs):
    pieces, out_ref, sems = refs[:-2], refs[-2], refs[-1]
    width = pieces[0].shape[1]
    copies = []
    for n, (offset, row, rows) in enumerate(places):
        source = lax.rem(lax.axis_index("kvh") + planes - offset, planes)
        at = pl.multiple_of(source * width, width)
        target = out_ref.at[pl.ds(row, rows), pl.ds(at, width)]
        copies.append(pltpu.make_async_copy(pieces[n].at[pl.ds(0, rows), :], target, sems.at[n]))
        copies[-1].start()
    for copy in copies:
        copy.wait()


def assemble(places, planes, pieces):
    width = pieces[0].shape[1]
    return pl.pallas_call(
        functools.partial(assemble_kernel, places, planes),
        out_shape=jax.ShapeDtypeStruct((BLK, width * planes), jnp.bfloat16),
        in_specs=[IN_VMEM] * len(pieces),
        out_specs=ANYWHERE,
        scratch_shapes=[pltpu.SemaphoreType.DMA((len(pieces),))],
        compiler_params=SMALL,
        cost_estimate=small_cost(2**23),
    )(*pieces)


def window_routes(stretches):
    chips = stretches // 2
    first, mixed, last = [], [], []
    for chip in range(chips):
        y, x = divmod(chip, 4)
        for core in range(2):
            first.append((2 * chip + core, (2 * chip + core + 2) % stretches))
        mixed.append((2 * chip, 2 * chip + 1))
        half_y = y + 1 if x == 2 else y
        half = (half_y * 4 + (x - 1) % 4) % chips
        target = (chip + 2) % chips
        mixed.append((2 * chip + 1, 2 * half))
        last.append((2 * half, 2 * target))
    return first, mixed, last


def exchange(parts, groups):
    return lax.all_to_all(parts, "ctx", split_axis=0, concat_axis=0, axis_index_groups=groups, tiled=True)


def add_up(parts):
    return jnp.sum(parts.astype(jnp.float32), axis=0).astype(jnp.bfloat16)


def spread(part, copies):
    return jnp.broadcast_to(part[None], (copies,) + part.shape)


def shards(query_states, key_states, value_states, verticals, slashes):
    blocks = key_states.shape[0] // BLK
    stretches = lax.axis_size("ctx")
    planes = lax.axis_size("kvh")
    key_value, picked = prepare(verticals, key_states, value_states)

    lines = stretches // ROW
    rows = [[y * ROW + g for g in range(ROW)] for y in range(lines)]
    columns_of = [[y * ROW + g for y in range(lines)] for g in range(ROW)]
    share = add_up(exchange(picked.reshape(ROW, -1, HD), rows))
    share = add_up(exchange(spread(share, lines), columns_of))

    first, mixed, last = window_routes(stretches)
    two_back = lax.ppermute(key_value, "ctx", first)
    halfway = lax.ppermute(key_value, "ctx", mixed)
    share, two_back = lax.optimization_barrier((share, two_back))
    swapped = lax.ppermute(two_back, "ctx", [(s, s ^ 1) for s in range(stretches)])
    onward = lax.ppermute(halfway, "ctx", last)

    columns = exchange(spread(share, ROW), rows).reshape(2, -1, HD)
    slots = plan(blocks, verticals, slashes)
    pool = make_pool(blocks, key_value, swapped, two_back, halfway, onward, columns)

    def attend(offsets, after):
        return attend_call(tuple(n % planes for n in offsets), blocks, slots, pool, query_states, after)

    def send(block, offset):
        return lax.ppermute(block, "kvh", [(s, (s + offset) % planes) for s in range(planes)])

    upper, bundle = attend((FAR_SIDE, BY_STEPS), [])
    after = [upper]
    upper = send(upper, FAR_SIDE)
    bundle = send(bundle, BY_STEPS)
    lower = send(bundle[BLK:], BY_STEPS)
    pieces = [upper, lower, bundle]
    places = [(FAR_SIDE, 0, HALF), (FAR_SIDE, HALF, HALF), (BY_STEPS % planes, 0, BLK)]
    arrived = {3: [bundle], 4: [upper]}
    for number, offset in enumerate(OFFSETS):
        (result,) = attend((offset,), after + arrived.get(number, []))
        after = [result]
        if offset:
            result = send(result, offset)
        if number == 0:
            arrived[5] = [result]
        pieces.append(result)
        places.append((offset % planes, 0, BLK))
    return assemble(tuple(places), planes, pieces)


def solution(mesh):
    return jax.shard_map(
        shards,
        mesh=mesh,
        in_specs=(
            P("ctx", "kvh"),
            P("ctx", "kvh"),
            P("ctx", "kvh"),
            P("kvh", None),
            P("kvh", None),
        ),
        out_specs=P(("ctx", "kvh"), None),
        check_vma=False,
    )
```
